512 devices in a mesh: dp: 64 (over y, z_lo, x), mp: 8 (over z_hi, core).
Axes of the slice: x: 4, y: 8, z: 8 (z_hi: 4, z_lo: 2; z = z_hi * 2 + z_lo), core: 2. Of those that a mesh axis runs over, the one named last changes fastest.
Arguments:
- grad_partials: bfloat16 [64, 64, 73728], P('dp', None, 'mp'), may hold values from -240 to 240
- master: float32 [64, 73728], P('dp', 'mp'), may hold values from -6 to 6
- row_state: float32 [64], P('dp'), may hold values from 10 to 10000
- col_state: float32 [73728], P('mp'), may hold values from 10 to 10000
Outputs:
- master_new: float32 [64, 73728], P('dp', 'mp')
- weight_full: bfloat16 [64, 73728], P(None, 'mp')
- row_new: float32 [64], P('dp')
- col_new: float32 [73728], P('mp')
The draws below stay inside these ranges and needn't reach their ends.
All inputs are finite; a program needn't handle non-finite values.
Results may differ from the reference program's by a relative error of at most 0.0013.
Values may be sent and summed in bfloat16 or wider, within the bound.
A program may use at most 64 MiB of HBM per device.

```python
import math
import jax
import jax.numpy as jnp
from jax import lax

FF = 73728
ROWS = 64
N_DP = 64


def draw_grad_partials(key, part):
    key = jax.random.fold_in(key, 11)
    first = jax.random.fold_in(key, 0)
    second = jax.random.fold_in(key, 1)
    fourth = jax.random.fold_in(key, 3)
    position = jnp.arange(ROWS, dtype=jnp.float32) / max(ROWS - 1, 1)
    row_scale = jnp.exp(math.log(3.0) * position + jax.random.uniform(first, (ROWS,), jnp.float32, 0.0, math.log(10.0)))
    col_scale = jnp.exp(jax.random.uniform(second, (FF,), jnp.float32, 0.0, math.log(10.0)))
    values = jnp.clip(jax.random.normal(fourth, (N_DP, ROWS, FF), jnp.float32), -6.0, 6.0)
    values = 0.125 * values * row_scale[None, :, None] * col_scale[None, None, :]
    return values.astype(jnp.bfloat16)


def steps_of(stream_key, shape, cuts, smallest, largest):
    factor_of = 1.0
    for dim, blocks in cuts:
        steps = jax.random.uniform(jax.random.fold_in(jax.random.fold_in(stream_key, 6), dim), (blocks,), jnp.float32, smallest / len(cuts), largest / len(cuts))
        factor_of = factor_of * jnp.repeat(jnp.exp(steps), shape[dim] // blocks).reshape((-1,) + (1,) * (len(shape) - 1 - dim))
    return factor_of


def bell_draw(key, extent, width, limit, pieces=(), held_as=jnp.bfloat16):
    result = width * jax.random.normal(key, extent, jnp.float32)
    if pieces:
        result = result * steps_of(key, extent, pieces, -0.22, 0.18)
    return jnp.clip(result, -limit, limit).astype(held_as)


def setup_inputs(seed: int = 0) -> dict:
    streams_of = jax.random.split(jax.random.key(seed), 5)
    grad_partials = draw_grad_partials(jax.random.fold_in(streams_of[4], 71), 0)
    master = bell_draw(streams_of[1], (ROWS, FF), 1.0, 6.0, ((0, 64), (1, 8)), jnp.float32)
    row_state = jnp.clip(jnp.exp(math.log(10000.0) - 6.9077553 * jax.random.uniform(streams_of[2], (ROWS,), jnp.float32) ** steps_of(streams_of[2], (ROWS,), ((0, 64),), -0.2, 0.2)), 10.0, 10000.0)
    col_state = jnp.clip(jnp.exp(math.log(10000.0) - 6.9077553 * jax.random.uniform(streams_of[3], (FF,), jnp.float32) ** steps_of(streams_of[3], (FF,), ((0, 8),), -0.2, 0.2)), 10.0, 10000.0)
    return dict(grad_partials=grad_partials, master=master, row_state=row_state, col_state=col_state)


decay_rate = 0.5
clip_level = 1.0
step_size = 0.5
tiny_term = 1e-30

def reference(grad_partials, master, row_state, col_state):
    gradient = lax.optimization_barrier(jnp.sum(grad_partials, axis=0, dtype=jnp.float32))
    square = gradient * gradient
    row_new = decay_rate * row_state + (1.0 - decay_rate) * (lax.optimization_barrier(jnp.sum(square, axis=1)) / FF + tiny_term)
    col_new = decay_rate * col_state + (1.0 - decay_rate) * (lax.optimization_barrier(jnp.sum(square, axis=0)) / ROWS + tiny_term)
    mean_row = jnp.sum(row_new) / ROWS
    update = gradient * lax.rsqrt(row_new[:, None] * col_new[None, :] / mean_row)
    energy = jnp.sum(update * update)
    scale = jnp.maximum(1.0, jnp.sqrt(energy / (ROWS * FF)) / clip_level)
    master_new = master - step_size * (update / scale)
    return (master_new, master_new.astype(jnp.bfloat16), row_new, col_new)
```

```python
import functools

import jax
import jax.numpy as jnp
from jax import lax
from jax.experimental import pallas as pl
from jax.experimental.pallas import tpu as pltpu
from jax.sharding import PartitionSpec as P

MESH = pl.DeviceIdType.MESH
LANES = 128

decay_rate = 0.5
clip_level = 1.0
step_size = 0.5
tiny_term = 1e-30


def kernel(
    ny,
    nk,
    nm,
    splits,
    grad_ref,
    master_ref,
    row_state_ref,
    col_state_ref,
    master_out,
    weight_out,
    row_out,
    col_out,
    parts,
    chunk_sum,
    tile_in,
    extra_in,
    master_rows,
    master_chunk,
    master_tile,
    master_extra,
    stat,
    weights,
    fresh_tile,
    fresh_extra,
    fresh_chunk,
    fresh_rows,
    col_chunk,
    local_sem,
    parts_send,
    parts_recv,
    tile_send,
    tile_recv,
    extra_send,
    extra_recv,
    mrow_send,
    mrow_recv,
    mtile_send,
    mtile_recv,
    mextra_send,
    mextra_recv,
    stat_send,
    stat_recv,
    w_send,
    w_recv,
    wx_send,
    wx_recv,
    f_send,
    f_recv,
    fx_send,
    fx_recv,
    c_send,
    c_recv,
    cx_send,
    cx_recv,
    wout_send,
    wout_recv,
    mout_send,
    mout_recv,
    cout_send,
    cout_recv,
):
    rows = ny * nk
    chunk = chunk_sum.shape[1]
    ff = chunk * nk * nm
    f32 = jnp.float32

    dp = lax.axis_index("dp")
    m = lax.axis_index("mp")
    y = dp // nk
    k = lax.rem(dp, nk)
    heavy = lax.rem(k + (ny // 2) * lax.rem(m, 2), ny)
    is_heavy = heavy == y
    heavy_at = lax.rem(heavy - y + ny, ny)

    def k_of(d):
        return lax.rem(k + d, nk)

    def k_peer(d):
        return (y * nk + k_of(d), m)

    def y_of(d):
        return lax.rem(y + d, ny)

    def y_dev(yy):
        return (yy * nk + k, m)

    def m_peer(d):
        return (dp, lax.rem(m + d, nm))

    def cols(start, width):
        return pl.ds(pl.multiple_of(start, LANES), width)

    def tile(t):
        return cols(t * LANES, LANES)

    def remote(src, dst, send, recv, device):
        return pltpu.make_async_remote_copy(
            src_ref=src, dst_ref=dst, send_sem=send, recv_sem=recv, device_id=device, device_id_type=MESH
        )

    bounds = []
    for s in range(len(splits)):
        first = sum(splits[:s])
        bounds.append((first, splits[s]))

    own = []
    for s, (first, count) in enumerate(bounds):
        c = pltpu.make_async_copy(
            grad_ref.at[:, cols(k * chunk + first * LANES, count * LANES)],
            parts.at[0, :, pl.ds(first * LANES, count * LANES)],
            local_sem.at[s],
        )
        c.start()
        own.append(c)
    own_master = pltpu.make_async_copy(
        master_ref.at[:, cols(k * chunk, chunk)], master_rows.at[k], local_sem.at[len(splits)]
    )
    own_master.start()

    barrier = pltpu.get_barrier_semaphore()
    peers = [k_peer(d) for d in range(1, nk)] + [y_dev(y_of(d)) for d in range(1, ny)] + [m_peer(d) for d in range(1, nm)]
    for device in peers:
        pl.semaphore_signal(barrier, inc=1, device_id=device, device_id_type=MESH)
    pl.semaphore_wait(barrier, len(peers))

    part_copy = {}
    for s, (first, count) in enumerate(bounds):
        for d in range(1, nk):
            c = remote(
                grad_ref.at[:, cols(k_of(d) * chunk + first * LANES, count * LANES)],
                parts.at[d, :, pl.ds(first * LANES, count * LANES)],
                parts_send.at[d, s],
                parts_recv.at[d, s],
                k_peer(d),
            )
            c.start()
            part_copy[d, s] = c
    mrow_copy = {}
    for d in range(1, nk):
        c = remote(
            master_ref.at[:, cols(k_of(d) * chunk, chunk)],
            master_rows.at[k],
            mrow_send.at[d],
            mrow_recv.at[d],
            k_peer(d),
        )
        c.start()
        mrow_copy[d] = c

    def tile_copy(d, t):
        return remote(chunk_sum.at[:, tile(t)], tile_in.at[d], tile_send.at[d], tile_recv.at[d], y_dev(y_of(d)))

    def extra_copy(d, yy):
        return remote(chunk_sum.at[:, pl.ds(ny * LANES, LANES)], extra_in.at[d], extra_send, extra_recv.at[d], y_dev(yy))

    for s, (first, count) in enumerate(bounds):
        where = pl.ds(first * LANES, count * LANES)
        own[s].wait()
        total = parts[0, :, where].astype(f32)
        for d in range(1, nk):
            part_copy[d, s].wait_recv()
            total = total + parts[d, :, where].astype(f32)
        chunk_sum[:, where] = total
        for t in range(first, first + count):
            if t < ny:

                @pl.when(y != t)
                def _():
                    tile_copy(lax.rem(t - y + ny, ny), t).start()
            else:

                @pl.when(jnp.logical_not(is_heavy))
                def _():
                    extra_copy(heavy_at, heavy).start()

    own_master.wait()
    for d in range(1, nk):
        mrow_copy[d].wait_recv()
    for r in range(nk):
        master_chunk[r : r + 1, :] = master_rows[r]
    my_rows = pl.ds(pl.multiple_of(y * nk, nk), nk)
    mtile_copy = {}
    for d in range(1, ny):
        c = remote(
            master_chunk.at[:, tile(y_of(d))],
            master_tile.at[my_rows, :],
            mtile_send.at[d],
            mtile_recv.at[d],
            y_dev(y_of(d)),
        )
        c.start()
        mtile_copy[d] = c
    master_tile[my_rows, :] = master_chunk[:, tile(y)]
    master_last = master_chunk.at[:, pl.ds(ny * LANES, LANES)]

    def mextra_copy(d, yy):
        return remote(master_last, master_extra.at[my_rows, :], mextra_send, mextra_recv.at[d], y_dev(yy))

    @pl.when(jnp.logical_not(is_heavy))
    def _():
        mextra_copy(heavy_at, heavy).start()
        master_extra[...] = jnp.zeros_like(master_extra)
        extra_in[0] = jnp.zeros((rows, LANES), f32)

    @pl.when(is_heavy)
    def _():
        master_extra[my_rows, :] = master_last[...]
        more = chunk_sum[:, pl.ds(ny * LANES, LANES)]
        for d in range(1, ny):
            extra_copy(d, heavy).wait_recv()
            more = more + extra_in[d]
        extra_in[0] = more

    gradient = chunk_sum[:, tile(y)]
    for d in range(1, ny):
        tile_copy(d, y_of(d)).wait_recv()
        gradient = gradient + tile_in[d]
    gradient_x = extra_in[0]

    square = gradient * gradient
    square_x = gradient_x * gradient_x

    def new_col(sq, t):
        state = col_state_ref[:, tile(k * (ny + 1) + t)]
        total = jnp.sum(sq, axis=0, keepdims=True)
        return decay_rate * state + (1.0 - decay_rate) * (total / rows + tiny_term)

    col_new = new_col(square, y)
    col_new_x = new_col(square_x, ny)
    half = gradient * lax.rsqrt(col_new)
    half_x = gradient_x * lax.rsqrt(col_new_x)
    both = jnp.concatenate([square + square_x, half * half + half_x * half_x], axis=0)
    sums = lax.dot_general(
        jnp.ones((8, LANES), f32),
        both,
        (((1,), (1,)), ((), ())),
        precision=lax.Precision.HIGHEST,
        preferred_element_type=f32,
    )

    def exchange(stage, n, peer, value):
        stat[stage, 0] = value
        copies = []
        for d in range(1, n):
            c = remote(
                stat.at[stage, 0], stat.at[stage, d], stat_send.at[stage, d], stat_recv.at[stage, d], peer(d)
            )
            c.start()
            copies.append(c)
        return copies

    def collect(stage, n, copies, value):
        for d in range(1, n):
            copies[d - 1].wait_recv()
            value = value + stat[stage, d]
        return value

    stat_copies = exchange(0, nm, m_peer, sums)
    pending = list(stat_copies)

    col_chunk[:, tile(y)] = col_new
    ccopy = []
    for d in range(1, ny):
        c = remote(col_chunk.at[:, tile(y)], col_chunk.at[:, tile(y)], c_send.at[d], c_recv.at[d], y_dev(y_of(d)))
        c.start()
        ccopy.append(c)

    def cx_copy(d):
        last = col_chunk.at[:, pl.ds(ny * LANES, LANES)]
        return remote(last, last, cx_send.at[d], cx_recv, y_dev(y_of(d)))

    @pl.when(is_heavy)
    def _():
        col_chunk[:, pl.ds(ny * LANES, LANES)] = col_new_x
        for d in range(1, ny):
            cx_copy(d).start()

    sums = collect(0, nm, stat_copies, sums)
    lane = lax.broadcasted_iota(jnp.int32, sums.shape, 1)
    line = lax.broadcasted_iota(jnp.int32, sums.shape, 0)
    state = jnp.where(lane == dp, jnp.broadcast_to(row_state_ref[...], sums.shape), 0.0)
    sums = jnp.where(line == 1, state, sums)
    stat_copies = exchange(1, nk, k_peer, sums)
    pending += stat_copies

    for d in range(1, ny):
        ccopy[d - 1].wait_recv()

    @pl.when(jnp.logical_not(is_heavy))
    def _():
        cx_copy(1).wait_recv()

    col_copies = []
    here = cols(k * chunk, chunk)
    for d in range(1, nk):
        c = remote(col_chunk, col_out.at[:, here], cout_send.at[d], cout_recv.at[d], k_peer(d))
        c.start()
        col_copies.append(c)
    own_col = pltpu.make_async_copy(col_chunk, col_out.at[:, here], local_sem.at[0])
    own_col.start()

    sums = collect(1, nk, stat_copies, sums)
    stat_copies = exchange(2, ny, lambda d: y_dev(y_of(d)), sums)
    pending += stat_copies
    for d in range(1, ny):
        mtile_copy[d].wait_recv()

    @pl.when(is_heavy)
    def _():
        for d in range(1, ny):
            mextra_copy(d, heavy).wait_recv()

    sums = collect(2, ny, stat_copies, sums)

    row_total = sums[0:1, :rows]
    update_total = sums[0:1, rows:]
    row_state = sums[1:2, :rows]
    row_new = decay_rate * row_state + (1.0 - decay_rate) * (row_total / ff + tiny_term)
    mean_row = jnp.sum(row_new, axis=1, keepdims=True) / rows
    energy = mean_row * jnp.sum(update_total / row_new, axis=1, keepdims=True)
    scale = jnp.maximum(1.0, jnp.sqrt(energy / (rows * ff)) / clip_level)
    factor = lax.rsqrt(row_new) * (step_size * jnp.sqrt(mean_row) / scale)
    eye = lax.broadcasted_iota(jnp.int32, (rows, rows), 0) == lax.broadcasted_iota(jnp.int32, (rows, rows), 1)
    factor = jnp.sum(jnp.where(eye, jnp.broadcast_to(factor, (rows, rows)), 0.0), axis=1, keepdims=True)
    fresh = master_tile[...] - factor * half
    fresh_x = master_extra[...] - factor * half_x
    mine = tile(y)
    last = pl.ds(ny * LANES, LANES)
    weights[:, mine] = fresh.astype(jnp.bfloat16)

    wcopy = []
    for d in range(1, ny):
        c = remote(weights.at[:, mine], weights.at[:, mine], w_send.at[d], w_recv.at[d], y_dev(y_of(d)))
        c.start()
        wcopy.append(c)

    def wx_copy(d):
        return remote(weights.at[:, last], weights.at[:, last], wx_send.at[d], wx_recv, y_dev(y_of(d)))

    def rows_of(d):
        return pl.ds(pl.multiple_of(y_of(d) * nk, nk), nk)

    def fx_copy(d):
        return remote(
            fresh_extra.at[rows_of(d), :], fresh_chunk.at[:, last], fx_send.at[d], fx_recv, y_dev(y_of(d))
        )

    @pl.when(is_heavy)
    def _():
        weights[:, last] = fresh_x.astype(jnp.bfloat16)
        for d in range(1, ny):
            wx_copy(d).start()

    fresh_tile[...] = fresh
    fcopy = []
    for d in range(1, ny):
        c = remote(
            fresh_tile.at[rows_of(d), :], fresh_chunk.at[:, mine], f_send.at[d], f_recv.at[d], y_dev(y_of(d))
        )
        c.start()
        fcopy.append(c)
    fresh_chunk[:, mine] = fresh_tile[rows_of(0), :]

    @pl.when(is_heavy)
    def _():
        fresh_extra[...] = fresh_x
        for d in range(1, ny):
            fx_copy(d).start()
        fresh_chunk[:, last] = fresh_extra[rows_of(0), :]

    full_lane = lax.broadcasted_iota(jnp.int32, row_new.shape, 1)
    row_out[...] = jnp.sum(jnp.where(full_lane == dp, row_new, 0.0), axis=1, keepdims=True)

    for d in range(1, ny):
        wcopy[d - 1].wait_recv()

    @pl.when(jnp.logical_not(is_heavy))
    def _():
        wx_copy(1).wait_recv()

    wout = []
    for d in range(1, nk):
        c = remote(weights, weight_out.at[:, here], wout_send.at[d], wout_recv.at[d], k_peer(d))
        c.start()
        wout.append(c)
    own_weight = pltpu.make_async_copy(weights, weight_out.at[:, here], local_sem.at[1])
    own_weight.start()

    for d in range(1, ny):
        fcopy[d - 1].wait_recv()

    @pl.when(jnp.logical_not(is_heavy))
    def _():
        fx_copy(1).wait_recv()

    for r in range(nk):
        fresh_rows[r] = fresh_chunk[r : r + 1, :]
    mout = []
    for d in range(1, nk):
        c = remote(fresh_rows.at[k_of(d)], master_out.at[:, here], mout_send.at[d], mout_recv.at[d], k_peer(d))
        c.start()
        mout.append(c)
    own_fresh = pltpu.make_async_copy(fresh_rows.at[k], master_out.at[:, here], local_sem.at[2])
    own_fresh.start()

    own_col.wait()
    own_weight.wait()
    own_fresh.wait()
    for group in (col_copies, wout, mout):
        for c in group:
            c.wait_recv()
    for c in list(part_copy.values()) + list(mrow_copy.values()) + list(mtile_copy.values()):
        c.wait_send()
    for d in range(1, ny):
        tile_copy(d, y_of(d)).wait_send()
    for group in (pending, ccopy, col_copies, wcopy, fcopy, wout, mout):
        for c in group:
            c.wait_send()

    @pl.when(jnp.logical_not(is_heavy))
    def _():
        extra_copy(heavy_at, heavy).wait_send()
        mextra_copy(heavy_at, heavy).wait_send()

    @pl.when(is_heavy)
    def _():
        for d in range(1, ny):
            cx_copy(d).wait_send()
            wx_copy(d).wait_send()
            fx_copy(d).wait_send()


def build(ny, nk, nm, splits):
    def per_device(grad_partials, master, row_state, col_state):
        grad = grad_partials[0]
        rows, width = grad.shape
        chunk = width // nk
        f32, bf16 = jnp.float32, jnp.bfloat16
        hbm = pl.BlockSpec(memory_space=pl.ANY)
        vmem = pl.BlockSpec(memory_space=pltpu.VMEM)
        dma = pltpu.SemaphoreType.DMA
        pair = lambda *n: [dma(n), dma(n)]
        out = pl.pallas_call(
            functools.partial(kernel, ny, nk, nm, splits),
            out_shape=(
                jax.ShapeDtypeStruct((1, width), f32),
                jax.ShapeDtypeStruct((rows, width), bf16),
                jax.ShapeDtypeStruct((1, 1), f32),
                jax.ShapeDtypeStruct((1, width), f32),
            ),
            in_specs=[hbm, hbm, vmem, vmem],
            out_specs=(hbm, hbm, vmem, hbm),
            scratch_shapes=[
                pltpu.VMEM((nk, rows, chunk), bf16),
                pltpu.VMEM((rows, chunk), f32),
                pltpu.VMEM((ny, rows, LANES), f32),
                pltpu.VMEM((ny, rows, LANES), f32),
                pltpu.VMEM((nk, 1, chunk), f32),
                pltpu.VMEM((nk, chunk), f32),
                pltpu.VMEM((rows, LANES), f32),
                pltpu.VMEM((rows, LANES), f32),
                pltpu.VMEM((3, max(ny, nk, nm), 8, 2 * rows), f32),
                pltpu.VMEM((rows, chunk), bf16),
                pltpu.VMEM((rows, LANES), f32),
                pltpu.VMEM((rows, LANES), f32),
                pltpu.VMEM((nk, chunk), f32),
                pltpu.VMEM((nk, 1, chunk), f32),
                pltpu.VMEM((1, chunk), f32),
                dma((len(splits) + 4,)),
                *pair(nk, len(splits)),
                *pair(ny),
                dma, dma((ny,)),
                *pair(nk),
                *pair(ny),
                dma, dma((ny,)),
                *pair(3, max(ny, nk, nm)),
                *pair(ny),
                dma((ny,)), dma,
                *pair(ny),
                dma((ny,)), dma,
                *pair(ny),
                dma((ny,)), dma,
                *pair(nk),
                *pair(nk),
                *pair(nk),
            ],
            compiler_params=pltpu.CompilerParams(
                collective_id=0, has_side_effects=True, vmem_limit_bytes=32 * 1024 * 1024
            ),
        )(grad, master, row_state.reshape(1, 1), col_state.reshape(1, width))
        master_new, weight_full, row_new, col_new = out
        return (master_new, weight_full, row_new.reshape(1), col_new.reshape(width))

    return per_device


def solution(mesh):
    in_specs = (P("dp", None, "mp"), P("dp", "mp"), P("dp"), P("mp"))
    out_specs = (P("dp", "mp"), P(None, "mp"), P("dp"), P("mp"))
    return jax.shard_map(
        build(8, 8, 8, (3, 3, 3)), mesh=mesh, in_specs=in_specs, out_specs=out_specs, check_vma=False
    )
```

```python
import functools

import jax
import jax.numpy as jnp
from jax import lax
from jax.experimental import pallas as pl
from jax.experimental.pallas import tpu as pltpu
from jax.sharding import PartitionSpec as P

MESH = pl.DeviceIdType.MESH
LANES = 128
F32, BF16 = jnp.float32, jnp.bfloat16

decay_rate = 0.5
clip_level = 1.0
step_size = 0.5
tiny_term = 1e-30


class Slots:
    def __init__(self):
        self.used = 0

    def take(self, n=1):
        self.used += n
        return self.used - n


def kernel(
    n,
    nm,
    splits,
    grad_ref,
    master_ref,
    row_state_ref,
    col_state_ref,
    master_out,
    weight_out,
    row_out,
    col_out,
    parts,
    chunk_sum,
    tile_in,
    extra_in,
    master_rows,
    master_full,
    half_full,
    side_tile,
    side_extra,
    side,
    side_send,
    side_in,
    stat,
    fresh_rows,
    col_chunk,
    col_state,
    local_sem,
    send_sem,
    recv_sem,
):
    rows, chunk = chunk_sum.shape
    ff = chunk * n * nm
    per_chunk = n + 1
    q = side_in.shape[1]
    top = rows - q

    dp = lax.axis_index("dp")
    m = lax.axis_index("mp")
    y = dp // n
    k = lax.rem(dp, n)
    shift = (n // 2) * lax.rem(m, 2)
    heavy = lax.rem(k + shift, n)
    is_heavy = heavy == y
    heavy_at = lax.rem(heavy - y + n, n)

    def chunk_of_extra(yy):
        return lax.rem(yy + shift, n)

    def k_of(d):
        return lax.rem(k + d, n)

    def y_of(d):
        return lax.rem(y + d, n)

    def k_peer(d):
        return (y * n + k_of(d), m)

    def y_dev(yy):
        return (yy * n + k, m)

    def y_peer(d):
        return y_dev(y_of(d))

    def m_peer(d):
        return (dp, lax.rem(m + d, nm))

    def cols(start, width):
        return pl.ds(pl.multiple_of(start, LANES), width)

    def tile(t):
        return cols(t * LANES, LANES)

    slots = Slots()
    sent = []

    def remote(src, dst, slot, device):
        return pltpu.make_async_remote_copy(
            src_ref=src,
            dst_ref=dst,
            send_sem=send_sem.at[slot],
            recv_sem=recv_sem.at[slot],
            device_id=device,
            device_id_type=MESH,
        )

    def start_all(make):
        base = slots.take(n)
        copies = []
        for d in range(1, n):
            c = make(base + d, d)
            c.start()
            copies.append(c)
        sent.extend(copies)
        return copies

    def arrived(copies):
        for c in copies:
            c.wait_recv()

    mine = tile(y)
    last = pl.ds(n * LANES, LANES)
    here = cols(k * chunk, chunk)
    my_rows = pl.ds(pl.multiple_of(y * n, n), n)

    bounds = [(sum(splits[:s]), splits[s]) for s in range(len(splits))]
    own = []
    for s, (first, count) in enumerate(bounds):
        c = pltpu.make_async_copy(
            grad_ref.at[:, cols(k * chunk + first * LANES, count * LANES)],
            parts.at[0, :, pl.ds(first * LANES, count * LANES)],
            local_sem.at[s],
        )
        c.start()
        own.append(c)
    own_master = pltpu.make_async_copy(master_ref.at[:, here], master_rows.at[k], local_sem.at[len(splits)])
    own_master.start()
    own_state = pltpu.make_async_copy(col_state_ref, col_state, local_sem.at[len(splits) + 1])
    own_state.start()

    barrier = pltpu.get_barrier_semaphore()
    peers = [k_peer(d) for d in range(1, n)] + [y_peer(d) for d in range(1, n)] + [m_peer(d) for d in range(1, nm)]
    for device in peers:
        pl.semaphore_signal(barrier, inc=1, device_id=device, device_id_type=MESH)
    pl.semaphore_wait(barrier, len(peers))

    mrow = start_all(
        lambda slot, d: remote(master_ref.at[:, cols(k_of(d) * chunk, chunk)], master_rows.at[k], slot, k_peer(d))
    )
    part = [
        start_all(
            lambda slot, d: remote(
                grad_ref.at[:, cols(k_of(d) * chunk + first * LANES, count * LANES)],
                parts.at[d, :, pl.ds(first * LANES, count * LANES)],
                slot,
                k_peer(d),
            )
        )
        for first, count in bounds
    ]
    own_master.wait()
    arrived(mrow)
    master_full[my_rows, :] = jnp.concatenate([master_rows[r] for r in range(n)], axis=0)
    mfull = start_all(
        lambda slot, d: remote(master_full.at[my_rows, :], master_full.at[my_rows, :], slot, y_peer(d))
    )

    tile_slot = slots.take(n)
    extra_slot = slots.take(n)

    def tile_copy(d, t):
        return remote(chunk_sum.at[:, tile(t)], tile_in.at[d], tile_slot + d, y_peer(d))

    def extra_copy(d):
        return remote(chunk_sum.at[:, last], extra_in.at[d], extra_slot + d, y_dev(heavy))

    for s, (first, count) in enumerate(bounds):
        where = pl.ds(first * LANES, count * LANES)
        own[s].wait()
        total = parts[0, :, where].astype(F32)
        for d in range(1, n):
            part[s][d - 1].wait_recv()
            total = total + parts[d, :, where].astype(F32)
        chunk_sum[:, where] = total
        for t in range(first, first + count):
            if t < n:

                @pl.when(y != t)
                def _():
                    tile_copy(lax.rem(t - y + n, n), t).start()
            else:

                @pl.when(jnp.logical_not(is_heavy))
                def _():
                    extra_copy(heavy_at).start()

    @pl.when(jnp.logical_not(is_heavy))
    def _():
        extra_in[0] = jnp.zeros((rows, LANES), F32)

    gradient = chunk_sum[:, mine]
    for d in range(1, n):
        tile_copy(d, y_of(d)).wait_recv()
        gradient = gradient + tile_in[d]

    @pl.when(is_heavy)
    def _():
        more = chunk_sum[:, last]
        for d in range(1, n):
            extra_copy(d).wait_recv()
            more = more + extra_in[d]
        extra_in[0] = more

    gradient_x = extra_in[0]

    own_state.wait()
    square = gradient * gradient
    square_x = gradient_x * gradient_x

    def new_col(sq, t):
        state = col_state[:, tile(k * per_chunk + t)]
        total = jnp.sum(sq, axis=0, keepdims=True)
        return decay_rate * state + (1.0 - decay_rate) * (total / rows + tiny_term)

    col_new = new_col(square, y)
    col_new_x = new_col(square_x, n)
    half = gradient * lax.rsqrt(col_new)
    half_x = gradient_x * lax.rsqrt(col_new_x)
    both = jnp.concatenate([square + square_x, half * half + half_x * half_x], axis=0)
    sums = lax.dot_general(
        jnp.ones((8, LANES), F32),
        both,
        (((1,), (1,)), ((), ())),
        precision=lax.Precision.HIGHEST,
        preferred_element_type=F32,
    )

    stat_slots = slots.take(3 * max(n, nm))

    def exchange(stage, members, peer, value):
        stat[stage, 0] = value
        copies = []
        for d in range(1, members):
            c = remote(
                stat.at[stage, 0], stat.at[stage, d], stat_slots + stage * max(n, nm) + d, peer(d)
            )
            c.start()
            copies.append(c)
        sent.extend(copies)
        return copies

    def collect(stage, copies, value):
        for d, c in enumerate(copies):
            c.wait_recv()
            value = value + stat[stage, d + 1]
        return value

    stat_copies = exchange(0, nm, m_peer, sums)

    half_full[:, mine] = half
    hcopy = start_all(lambda slot, d: remote(half_full.at[:, mine], half_full.at[:, mine], slot, y_peer(d)))
    hx_send = slots.take(n)
    hx_recv = slots.take()

    def one_to_all(src, dst, send, recv, device):
        return pltpu.make_async_remote_copy(
            src_ref=src,
            dst_ref=dst,
            send_sem=send_sem.at[send],
            recv_sem=recv_sem.at[recv],
            device_id=device,
            device_id_type=MESH,
        )

    def hx_copy(d):
        return one_to_all(half_full.at[:, last], half_full.at[:, last], hx_send + d, hx_recv, y_peer(d))

    @pl.when(is_heavy)
    def _():
        half_full[:, last] = half_x
        for d in range(1, n):
            hx_copy(d).start()

    col_chunk[:, mine] = col_new
    ccopy = start_all(lambda slot, d: remote(col_chunk.at[:, mine], col_chunk.at[:, mine], slot, y_peer(d)))
    cx_send = slots.take(n)
    cx_recv = slots.take()

    def cx_copy(d):
        return one_to_all(col_chunk.at[:, last], col_chunk.at[:, last], cx_send + d, cx_recv, y_peer(d))

    @pl.when(is_heavy)
    def _():
        col_chunk[:, last] = col_new_x
        for d in range(1, n):
            cx_copy(d).start()

    arrived(mfull)
    side_tile[0] = half[top:, :]
    side_tile[1] = master_full[top:, mine]
    scopy = start_all(lambda slot, d: remote(side_tile, side.at[k], slot, k_peer(d)))
    side[k] = side_tile[...]
    sx_send = slots.take(n)
    sx_recv = slots.take()

    def sx_copy(d):
        return one_to_all(side_extra, side.at[n], sx_send + d, sx_recv, k_peer(d))

    @pl.when(is_heavy)
    def _():
        side_extra[0] = half_x[top:, :]
        side_extra[1] = master_full[top:, last]
        for d in range(1, n):
            sx_copy(d).start()
        side[n] = side_extra[...]

    sums = collect(0, stat_copies, sums)
    lane = lax.broadcasted_iota(jnp.int32, sums.shape, 1)
    line = lax.broadcasted_iota(jnp.int32, sums.shape, 0)
    state = jnp.where(lane == dp, jnp.broadcast_to(row_state_ref[...], sums.shape), 0.0)
    sums = jnp.where(line == 1, state, sums)
    stat_copies = exchange(1, n, k_peer, sums)

    arrived(ccopy)

    @pl.when(jnp.logical_not(is_heavy))
    def _():
        cx_copy(1).wait_recv()

    sums = collect(1, stat_copies, sums)
    stat_copies = exchange(2, n, y_peer, sums)

    ocopy = start_all(lambda slot, d: remote(col_chunk, col_out.at[:, here], slot, k_peer(d)))
    col_out[:, here] = col_chunk[...]
    arrived(hcopy)
    arrived(scopy)

    @pl.when(jnp.logical_not(is_heavy))
    def _():
        hx_copy(1).wait_recv()
        sx_copy(1).wait_recv()

    sums = collect(2, stat_copies, sums)

    row_total = sums[0:1, :rows]
    update_total = sums[0:1, rows:]
    row_state = sums[1:2, :rows]
    row_new = decay_rate * row_state + (1.0 - decay_rate) * (row_total / ff + tiny_term)
    mean_row = jnp.sum(row_new, axis=1, keepdims=True) / rows
    energy = mean_row * jnp.sum(update_total / row_new, axis=1, keepdims=True)
    scale = jnp.maximum(1.0, jnp.sqrt(energy / (rows * ff)) / clip_level)
    factor = lax.rsqrt(row_new) * (step_size * jnp.sqrt(mean_row) / scale)
    eye = lax.broadcasted_iota(jnp.int32, (rows, rows), 0) == lax.broadcasted_iota(jnp.int32, (rows, rows), 1)
    factor = jnp.sum(jnp.where(eye, jnp.broadcast_to(factor, (rows, rows)), 0.0), axis=1, keepdims=True)

    for first, count in bounds:
        where = pl.ds(first * LANES, count * LANES)
        fresh = master_full[:top, where] - factor[:top] * half_full[:top, where]
        weight_out[:top, cols(k * chunk + first * LANES, count * LANES)] = fresh.astype(BF16)
    upper = weight_out.at[pl.ds(0, top), here]
    wcopy = start_all(lambda slot, d: remote(upper, upper, slot, k_peer(d)))

    def side_tile_at(j, yy):
        chunk_at = j if j < n else chunk_of_extra(yy)
        return tile(chunk_at * per_chunk + (yy if j < n else n))

    for j in range(per_chunk):
        fresh = (side[j, 1] - factor[top:] * side[j, 0]).astype(BF16)
        side_send[:, pl.ds(j * LANES, LANES)] = fresh
        weight_out[top:, side_tile_at(j, y)] = fresh
    ucopy = start_all(lambda slot, d: remote(side_send, side_in.at[d], slot, y_peer(d)))

    pick = lax.broadcasted_iota(jnp.int32, (n, rows), 1) - y * n == lax.broadcasted_iota(jnp.int32, (n, rows), 0)
    row_factor = lax.rsqrt(row_new) * (step_size * jnp.sqrt(mean_row) / scale)
    row_factor = jnp.sum(jnp.where(pick, jnp.broadcast_to(row_factor, (n, rows)), 0.0), axis=1, keepdims=True)
    fresh = master_full[my_rows, :] - row_factor * half_full[my_rows, :]
    for r in range(n):
        fresh_rows[r] = fresh[r : r + 1, :]
    fcopy = start_all(lambda slot, d: remote(fresh_rows.at[k_of(d)], master_out.at[:, here], slot, k_peer(d)))
    master_out[:, here] = fresh_rows[k]

    full_lane = lax.broadcasted_iota(jnp.int32, row_new.shape, 1)
    row_out[...] = jnp.sum(jnp.where(full_lane == dp, row_new, 0.0), axis=1, keepdims=True)

    for d in range(1, n):
        ucopy[d - 1].wait_recv()
        yy = lax.rem(y - d + n, n)
        for j in range(per_chunk):
            weight_out[top:, side_tile_at(j, yy)] = side_in[d, :, pl.ds(j * LANES, LANES)]
    arrived(ocopy)
    arrived(fcopy)
    arrived(wcopy)

    for c in sent:
        c.wait_send()
    for d in range(1, n):
        tile_copy(d, y_of(d)).wait_send()

    @pl.when(jnp.logical_not(is_heavy))
    def _():
        extra_copy(heavy_at).wait_send()

    @pl.when(is_heavy)
    def _():
        for d in range(1, n):
            hx_copy(d).wait_send()
            cx_copy(d).wait_send()
            sx_copy(d).wait_send()


def build(n, nm, splits):
    def per_device(grad_partials, master, row_state, col_state):
        grad = grad_partials[0]
        rows, width = grad.shape
        chunk = width // n
        quarter = rows // 4
        hbm = pl.BlockSpec(memory_space=pltpu.HBM)
        vmem = pl.BlockSpec(memory_space=pltpu.VMEM)
        dma = pltpu.SemaphoreType.DMA

        def in_hbm(a):
            return pltpu.with_memory_space_constraint(a, pltpu.HBM)

        out = pl.pallas_call(
            functools.partial(kernel, n, nm, splits),
            out_shape=(
                jax.ShapeDtypeStruct((1, width), F32),
                jax.ShapeDtypeStruct((rows, width), BF16),
                jax.ShapeDtypeStruct((1, 1), F32),
                jax.ShapeDtypeStruct((1, width), F32),
            ),
            in_specs=[hbm, hbm, vmem, hbm],
            out_specs=(vmem, vmem, vmem, vmem),
            scratch_shapes=[
                pltpu.VMEM((n, rows, chunk), BF16),
                pltpu.VMEM((rows, chunk), F32),
                pltpu.VMEM((n, rows, LANES), F32),
                pltpu.VMEM((n, rows, LANES), F32),
                pltpu.VMEM((n, 1, chunk), F32),
                pltpu.VMEM((rows, chunk), F32),
                pltpu.VMEM((rows, chunk), F32),
                pltpu.VMEM((2, quarter, LANES), F32),
                pltpu.VMEM((2, quarter, LANES), F32),
                pltpu.VMEM((n + 1, 2, quarter, LANES), F32),
                pltpu.VMEM((quarter, chunk), BF16),
                pltpu.VMEM((n, quarter, chunk), BF16),
                pltpu.VMEM((3, max(n, nm), 8, 2 * rows), F32),
                pltpu.VMEM((n, 1, chunk), F32),
                pltpu.VMEM((1, chunk), F32),
                pltpu.VMEM((1, width), F32),
                dma((len(splits) + 2,)),
                dma((256,)),
                dma((256,)),
            ],
            compiler_params=pltpu.CompilerParams(
                collective_id=0, has_side_effects=True, vmem_limit_bytes=32 * 1024 * 1024
            ),
        )(in_hbm(grad), in_hbm(master), row_state.reshape(1, 1), in_hbm(col_state.reshape(1, width)))
        master_new, weight_full, row_new, col_new = out
        return (master_new, weight_full, row_new.reshape(1), col_new.reshape(width))

    return per_device


def solution(mesh):
    in_specs = (P("dp", None, "mp"), P("dp", "mp"), P("dp"), P("mp"))
    out_specs = (P("dp", "mp"), P(None, "mp"), P("dp"), P("mp"))
    return jax.shard_map(
        build(8, 8, (3, 3, 3)), mesh=mesh, in_specs=in_specs, out_specs=out_specs, check_vma=False
    )
```

```python
import functools

import jax
import jax.numpy as jnp
from jax import lax
from jax.experimental import pallas as pl
from jax.experimental.pallas import tpu as pltpu
from jax.sharding import PartitionSpec as P

MESH = pl.DeviceIdType.MESH
LANES = 128
F32, BF16 = jnp.float32, jnp.bfloat16

decay_rate = 0.5
clip_level = 1.0
step_size = 0.5
tiny_term = 1e-30


class Slots:
    def __init__(self):
        self.used = 0

    def take(self, n=1):
        self.used += n
        return self.used - n


def kernel(
    n,
    nm,
    splits,
    grad_ref,
    master_ref,
    row_state_ref,
    col_state_ref,
    master_out,
    weight_out,
    row_out,
    col_out,
    parts,
    chunk_sum,
    tile_in,
    extra_in,
    master_rows,
    master_full,
    half_full,
    side_tile,
    side_extra,
    side,
    side_send,
    side_in,
    stat,
    fresh_rows,
    col_chunk,
    col_state,
    local_sem,
    send_sem,
    recv_sem,
):
    rows, chunk = chunk_sum.shape
    ff = chunk * n * nm
    per_chunk = n + 1
    q = side_in.shape[1]
    top = rows - q

    dp = lax.axis_index("dp")
    m = lax.axis_index("mp")
    y = dp // n
    k = lax.rem(dp, n)
    shift = (n // 2) * lax.rem(m, 2)
    heavy = lax.rem(k + shift, n)
    is_heavy = heavy == y
    heavy_at = lax.rem(heavy - y + n, n)

    def chunk_of_extra(yy):
        return lax.rem(yy + shift, n)

    def k_of(d):
        return lax.rem(k + d, n)

    def y_of(d):
        return lax.rem(y + d, n)

    def k_peer(d):
        return (y * n + k_of(d), m)

    def y_dev(yy):
        return (yy * n + k, m)

    def y_peer(d):
        return y_dev(y_of(d))

    def m_peer(d):
        return (dp, lax.rem(m + d, nm))

    def cols(start, width):
        return pl.ds(pl.multiple_of(start, LANES), width)

    def tile(t):
        return cols(t * LANES, LANES)

    slots = Slots()
    sent = []

    def remote(src, dst, slot, device):
        return pltpu.make_async_remote_copy(
            src_ref=src,
            dst_ref=dst,
            send_sem=send_sem.at[slot],
            recv_sem=recv_sem.at[slot],
            device_id=device,
            device_id_type=MESH,
        )

    def start_all(whole, make):
        slot = slots.take()
        for d in range(1, n):
            make(slot, d).start()
        group = remote(whole, whole, slot, k_peer(1))
        sent.append(group)
        return group

    others = pl.ds(1, n - 1)
    seven = pl.ds(0, n - 1)
    seven_tiles = pl.ds(0, (n - 1) * LANES)
    seven_chunks = pl.ds(0, (n - 1) * chunk)

    mine = tile(y)
    last = pl.ds(n * LANES, LANES)
    here = cols(k * chunk, chunk)
    my_rows = pl.ds(pl.multiple_of(y * n, n), n)

    bounds = [(sum(splits[:s]), splits[s]) for s in range(len(splits))]
    own = []
    for s, (first, count) in enumerate(bounds):
        c = pltpu.make_async_copy(
            grad_ref.at[:, cols(k * chunk + first * LANES, count * LANES)],
            parts.at[0, :, pl.ds(first * LANES, count * LANES)],
            local_sem.at[s],
        )
        c.start()
        own.append(c)
    own_master = pltpu.make_async_copy(master_ref.at[:, here], master_rows.at[k], local_sem.at[len(splits)])
    own_master.start()
    own_state = pltpu.make_async_copy(col_state_ref, col_state, local_sem.at[len(splits) + 1])
    own_state.start()

    barrier = pltpu.get_barrier_semaphore()
    peers = [k_peer(d) for d in range(1, n)] + [y_peer(d) for d in range(1, n)] + [m_peer(d) for d in range(1, nm)]
    for device in peers:
        pl.semaphore_signal(barrier, inc=1, device_id=device, device_id_type=MESH)
    pl.semaphore_wait(barrier, len(peers))

    mrow = start_all(
        master_rows.at[seven],
        lambda slot, d: remote(master_ref.at[:, cols(k_of(d) * chunk, chunk)], master_rows.at[k], slot, k_peer(d))
    )
    part = [
        start_all(
            parts.at[others, :, pl.ds(first * LANES, count * LANES)],
            lambda slot, d: remote(
                grad_ref.at[:, cols(k_of(d) * chunk + first * LANES, count * LANES)],
                parts.at[d, :, pl.ds(first * LANES, count * LANES)],
                slot,
                k_peer(d),
            )
        )
        for first, count in bounds
    ]
    own_master.wait()
    mrow.wait_recv()
    master_full[my_rows, :] = jnp.concatenate([master_rows[r] for r in range(n)], axis=0)
    mfull = start_all(
        master_full.at[pl.ds(0, rows - n), :],
        lambda slot, d: remote(master_full.at[my_rows, :], master_full.at[my_rows, :], slot, y_peer(d))
    )

    tile_slot = slots.take()
    extra_slot = slots.take()
    tiles_in = remote(tile_in.at[others], tile_in.at[others], tile_slot, k_peer(1))
    extras_in = remote(extra_in.at[others], extra_in.at[others], extra_slot, k_peer(1))

    def tile_copy(d, t):
        return remote(chunk_sum.at[:, tile(t)], tile_in.at[d], tile_slot, y_peer(d))

    def extra_copy(d):
        return remote(chunk_sum.at[:, last], extra_in.at[d], extra_slot, y_dev(heavy))

    for s, (first, count) in enumerate(bounds):
        where = pl.ds(first * LANES, count * LANES)
        own[s].wait()
        part[s].wait_recv()
        total = parts[0, :, where].astype(F32)
        for d in range(1, n):
            total = total + parts[d, :, where].astype(F32)
        chunk_sum[:, where] = total
        for t in range(first, first + count):
            if t < n:

                @pl.when(y != t)
                def _():
                    tile_copy(lax.rem(t - y + n, n), t).start()
            else:

                @pl.when(jnp.logical_not(is_heavy))
                def _():
                    extra_copy(heavy_at).start()

    @pl.when(jnp.logical_not(is_heavy))
    def _():
        extra_in[0] = jnp.zeros((rows, LANES), F32)

    tiles_in.wait_recv()
    gradient = chunk_sum[:, mine]
    for d in range(1, n):
        gradient = gradient + tile_in[d]

    @pl.when(is_heavy)
    def _():
        extras_in.wait_recv()
        more = chunk_sum[:, last]
        for d in range(1, n):
            more = more + extra_in[d]
        extra_in[0] = more

    gradient_x = extra_in[0]

    own_state.wait()
    square = gradient * gradient
    square_x = gradient_x * gradient_x

    def new_col(sq, t):
        state = col_state[:, tile(k * per_chunk + t)]
        total = jnp.sum(sq, axis=0, keepdims=True)
        return decay_rate * state + (1.0 - decay_rate) * (total / rows + tiny_term)

    col_new = new_col(square, y)
    col_new_x = new_col(square_x, n)
    half = gradient * lax.rsqrt(col_new)
    half_x = gradient_x * lax.rsqrt(col_new_x)
    both = jnp.concatenate([square + square_x, half * half + half_x * half_x], axis=0)
    sums = lax.dot_general(
        jnp.ones((8, LANES), F32),
        both,
        (((1,), (1,)), ((), ())),
        precision=lax.Precision.HIGHEST,
        preferred_element_type=F32,
    )

    def exchange(stage, members, peer, value):
        stat[stage, 0] = value
        slot = slots.take()
        for d in range(1, members):
            remote(stat.at[stage, 0], stat.at[stage, d], slot, peer(d)).start()
        if members == 1:
            return None
        whole = stat.at[stage, pl.ds(1, members - 1)]
        group = remote(whole, whole, slot, k_peer(1))
        sent.append(group)
        return group

    def collect(stage, members, group, value):
        if group is not None:
            group.wait_recv()
        for d in range(1, members):
            value = value + stat[stage, d]
        return value

    lane = lax.broadcasted_iota(jnp.int32, sums.shape, 1)
    line = lax.broadcasted_iota(jnp.int32, sums.shape, 0)
    state = jnp.where((lane == dp) & (m == 0), jnp.broadcast_to(row_state_ref[...], sums.shape), 0.0)
    sums = jnp.where(line == 1, state, sums)
    stat_group = exchange(0, n, y_peer, sums)

    half_full[:, mine] = half
    half_mine = half_full.at[:, mine]
    half_last = half_full.at[:, last]
    h_slot = slots.take()
    hx_slot = slots.take()
    hcopy = remote(half_full.at[:, seven_tiles], half_full.at[:, seven_tiles], h_slot, y_peer(1))
    sent.append(hcopy)

    @pl.when(is_heavy)
    def _():
        half_full[:, last] = half_x

    col_chunk[:, mine] = col_new
    ccopy = start_all(
        col_chunk.at[:, seven_tiles],
        lambda slot, d: remote(col_chunk.at[:, mine], col_chunk.at[:, mine], slot, y_peer(d)),
    )
    col_last = col_chunk.at[:, last]
    cx_slot = slots.take()

    @pl.when(is_heavy)
    def _():
        col_chunk[:, last] = col_new_x
        for d in range(1, n):
            remote(col_last, col_last, cx_slot, y_peer(d)).start()

    mfull.wait_recv()
    side_tile[0] = half[top:, :]
    side_tile[1] = master_full[top:, mine]
    scopy = start_all(side.at[seven], lambda slot, d: remote(side_tile, side.at[k], slot, k_peer(d)))
    side[k] = side_tile[...]
    sx_slot = slots.take()

    @pl.when(is_heavy)
    def _():
        side_extra[0] = half_x[top:, :]
        side_extra[1] = master_full[top:, last]
        for d in range(1, n):
            remote(side_extra, side.at[n], sx_slot, k_peer(d)).start()
        side[n] = side_extra[...]

    sums = collect(0, n, stat_group, sums)
    stat_group = exchange(1, nm, m_peer, sums)
    for d in range(1, n):
        remote(half_mine, half_mine, h_slot, y_peer(d)).start()

    @pl.when(is_heavy)
    def _():
        for d in range(1, n):
            remote(half_last, half_last, hx_slot, y_peer(d)).start()


    ccopy.wait_recv()

    @pl.when(jnp.logical_not(is_heavy))
    def _():
        remote(col_last, col_last, cx_slot, y_peer(1)).wait_recv()

    ocopy = start_all(
        col_out.at[:, seven_chunks],
        lambda slot, d: remote(col_chunk, col_out.at[:, here], slot, k_peer(d)),
    )
    col_out[:, here] = col_chunk[...]
    sums = collect(1, nm, stat_group, sums)
    stat_group = exchange(2, n, k_peer, sums)

    hcopy.wait_recv()
    scopy.wait_recv()

    @pl.when(jnp.logical_not(is_heavy))
    def _():
        remote(half_last, half_last, hx_slot, y_peer(1)).wait_recv()
        remote(side_extra, side_extra, sx_slot, k_peer(1)).wait_recv()

    sums = collect(2, n, stat_group, sums)

    row_total = sums[0:1, :rows]
    update_total = sums[0:1, rows:]
    row_state = sums[1:2, :rows]
    row_new = decay_rate * row_state + (1.0 - decay_rate) * (row_total / ff + tiny_term)
    mean_row = jnp.sum(row_new, axis=1, keepdims=True) / rows
    energy = mean_row * jnp.sum(update_total / row_new, axis=1, keepdims=True)
    scale = jnp.maximum(1.0, jnp.sqrt(energy / (rows * ff)) / clip_level)
    factor = lax.rsqrt(row_new) * (step_size * jnp.sqrt(mean_row) / scale)
    eye = lax.broadcasted_iota(jnp.int32, (rows, rows), 0) == lax.broadcasted_iota(jnp.int32, (rows, rows), 1)
    factor = jnp.sum(jnp.where(eye, jnp.broadcast_to(factor, (rows, rows)), 0.0), axis=1, keepdims=True)

    for first, count in bounds:
        where = pl.ds(first * LANES, count * LANES)
        fresh = master_full[:top, where] - factor[:top] * half_full[:top, where]
        weight_out[:top, cols(k * chunk + first * LANES, count * LANES)] = fresh.astype(BF16)
    upper = weight_out.at[pl.ds(0, top), here]
    wcopy = start_all(weight_out.at[pl.ds(0, top), seven_chunks], lambda slot, d: remote(upper, upper, slot, k_peer(d)))

    def side_tile_at(j, yy):
        chunk_at = j if j < n else chunk_of_extra(yy)
        return tile(chunk_at * per_chunk + (yy if j < n else n))

    for j in range(per_chunk):
        fresh = (side[j, 1] - factor[top:] * side[j, 0]).astype(BF16)
        side_send[:, pl.ds(j * LANES, LANES)] = fresh
        weight_out[top:, side_tile_at(j, y)] = fresh
    ucopy = start_all(side_in.at[others], lambda slot, d: remote(side_send, side_in.at[d], slot, y_peer(d)))

    pick = lax.broadcasted_iota(jnp.int32, (n, rows), 1) - y * n == lax.broadcasted_iota(jnp.int32, (n, rows), 0)
    row_factor = lax.rsqrt(row_new) * (step_size * jnp.sqrt(mean_row) / scale)
    row_factor = jnp.sum(jnp.where(pick, jnp.broadcast_to(row_factor, (n, rows)), 0.0), axis=1, keepdims=True)
    fresh = master_full[my_rows, :] - row_factor * half_full[my_rows, :]
    for r in range(n):
        fresh_rows[r] = fresh[r : r + 1, :]
    fcopy = start_all(master_out.at[:, seven_chunks], lambda slot, d: remote(fresh_rows.at[k_of(d)], master_out.at[:, here], slot, k_peer(d)))
    master_out[:, here] = fresh_rows[k]

    full_lane = lax.broadcasted_iota(jnp.int32, row_new.shape, 1)
    row_out[...] = jnp.sum(jnp.where(full_lane == dp, row_new, 0.0), axis=1, keepdims=True)

    ucopy.wait_recv()
    for d in range(1, n):
        yy = lax.rem(y - d + n, n)
        for j in range(per_chunk):
            weight_out[top:, side_tile_at(j, yy)] = side_in[d, :, pl.ds(j * LANES, LANES)]
    ocopy.wait_recv()
    fcopy.wait_recv()
    wcopy.wait_recv()

    for group in sent:
        group.wait_send()
    tiles_in.wait_send()

    @pl.when(jnp.logical_not(is_heavy))
    def _():
        extra_copy(heavy_at).wait_send()

    @pl.when(is_heavy)
    def _():
        remote(half_full.at[:, seven_tiles], half_full.at[:, seven_tiles], hx_slot, y_peer(1)).wait_send()
        remote(col_chunk.at[:, seven_tiles], col_chunk.at[:, seven_tiles], cx_slot, y_peer(1)).wait_send()
        remote(side.at[seven], side.at[seven], sx_slot, k_peer(1)).wait_send()


def writer(*refs):
    *pairs, sem = refs
    count = len(pairs) // 2
    copies = [pltpu.make_async_copy(pairs[i], pairs[count + i], sem.at[i]) for i in range(count)]
    for c in copies:
        c.start()
    for c in copies:
        c.wait()


def build(n, nm, splits):
    def per_device(grad_partials, master, row_state, col_state):
        grad = grad_partials[0]
        rows, width = grad.shape
        chunk = width // n
        quarter = rows // 4
        hbm = pl.BlockSpec(memory_space=pltpu.HBM)
        vmem = pl.BlockSpec(memory_space=pltpu.VMEM)
        dma = pltpu.SemaphoreType.DMA

        def in_hbm(a):
            return pltpu.with_memory_space_constraint(a, pltpu.HBM)

        out = pl.pallas_call(
            functools.partial(kernel, n, nm, splits),
            out_shape=(
                jax.ShapeDtypeStruct((1, width), F32),
                jax.ShapeDtypeStruct((rows, width), BF16),
                jax.ShapeDtypeStruct((1, 1), F32),
                jax.ShapeDtypeStruct((1, width), F32),
            ),
            in_specs=[hbm, hbm, vmem, hbm],
            out_specs=(vmem, vmem, vmem, vmem),
            scratch_shapes=[
                pltpu.VMEM((n, rows, chunk), BF16),
                pltpu.VMEM((rows, chunk), F32),
                pltpu.VMEM((n, rows, LANES), F32),
                pltpu.VMEM((n, rows, LANES), F32),
                pltpu.VMEM((n, 1, chunk), F32),
                pltpu.VMEM((rows, chunk), F32),
                pltpu.VMEM((rows, chunk), F32),
                pltpu.VMEM((2, quarter, LANES), F32),
                pltpu.VMEM((2, quarter, LANES), F32),
                pltpu.VMEM((n + 1, 2, quarter, LANES), F32),
                pltpu.VMEM((quarter, chunk), BF16),
                pltpu.VMEM((n, quarter, chunk), BF16),
                pltpu.VMEM((3, max(n, nm), 8, 2 * rows), F32),
                pltpu.VMEM((n, 1, chunk), F32),
                pltpu.VMEM((1, chunk), F32),
                pltpu.VMEM((1, width), F32),
                dma((len(splits) + 2,)),
                dma((24,)),
                dma((24,)),
            ],
            compiler_params=pltpu.CompilerParams(
                collective_id=0, has_side_effects=True, vmem_limit_bytes=32 * 1024 * 1024
            ),
        )(in_hbm(grad), in_hbm(master), row_state.reshape(1, 1), in_hbm(col_state.reshape(1, width)))
        master_new, weight_full, row_new, col_new = pl.pallas_call(
            writer,
            out_shape=tuple(jax.ShapeDtypeStruct(a.shape, a.dtype) for a in out),
            in_specs=[pl.BlockSpec(memory_space=pl.ANY)] * len(out),
            out_specs=tuple([hbm] * len(out)),
            scratch_shapes=[dma((len(out),))],
            compiler_params=pltpu.CompilerParams(vmem_limit_bytes=1024 * 1024),
        )(*out)
        return (master_new, weight_full, row_new.reshape(1), col_new.reshape(width))

    return per_device


def solution(mesh):
    in_specs = (P("dp", None, "mp"), P("dp", "mp"), P("dp"), P("mp"))
    out_specs = (P("dp", "mp"), P(None, "mp"), P("dp"), P("mp"))
    return jax.shard_map(
        build(8, 8, (4, 4, 1)), mesh=mesh, in_specs=in_specs, out_specs=out_specs, check_vma=False
    )
```

```python
import functools

import jax
import jax.numpy as jnp
from jax import lax
from jax.experimental import pallas as pl
from jax.experimental.pallas import tpu as pltpu
from jax.sharding import PartitionSpec as P

MESH = pl.DeviceIdType.MESH
LANES = 128
F32, BF16 = jnp.float32, jnp.bfloat16

decay_rate = 0.5
clip_level = 1.0
step_size = 0.5
tiny_term = 1e-30


class Slots:
    def __init__(self):
        self.used = 0

    def take(self, n=1):
        self.used += n
        return self.used - n


def kernel(
    n,
    nm,
    splits,
    grad_ref,
    master_ref,
    row_state_ref,
    col_state_ref,
    master_out,
    weight_out,
    row_out,
    col_out,
    parts,
    chunk_sum,
    tile_in,
    extra_parts,
    extra_sum,
    extra_in,
    master_rows,
    master_full,
    half_full,
    side_tile,
    side_extra,
    side,
    side_send,
    side_in,
    stat,
    fresh_rows,
    col_chunk,
    col_state,
    local_sem,
    send_sem,
    recv_sem,
):
    rows, chunk = chunk_sum.shape
    ff = chunk * n * nm
    per_chunk = n + 1
    q = side_in.shape[1]
    top = rows - q

    dp = lax.axis_index("dp")
    m = lax.axis_index("mp")
    y = dp // n
    k = lax.rem(dp, n)
    shift = (n // 2) * lax.rem(m, 2)
    is_heavy = lax.rem(k + shift, n) == y

    def chunk_of_extra(yy):
        return lax.rem(yy + shift, n)

    y_top = top // n
    lower = y >= y_top
    heavy_at = lax.rem(chunk_of_extra(y) - k + n, n)

    def k_of(d):
        return lax.rem(k + d, n)

    def y_of(d):
        return lax.rem(y + d, n)

    def k_peer(d):
        return (y * n + k_of(d), m)

    def y_dev(yy):
        return (yy * n + k, m)

    def y_peer(d):
        return y_dev(y_of(d))

    def m_peer(d):
        return (dp, lax.rem(m + d, nm))

    def cols(start, width):
        return pl.ds(pl.multiple_of(start, LANES), width)

    def tile(t):
        return cols(t * LANES, LANES)

    slots = Slots()
    sent = []

    def remote(src, dst, slot, device):
        return pltpu.make_async_remote_copy(
            src_ref=src,
            dst_ref=dst,
            send_sem=send_sem.at[slot],
            recv_sem=recv_sem.at[slot],
            device_id=device,
            device_id_type=MESH,
        )

    def start_all(whole, make):
        slot = slots.take()
        for d in range(1, n):
            make(slot, d).start()
        group = remote(whole, whole, slot, k_peer(1))
        sent.append(group)
        return group

    def whole_of(ref, slot):
        return remote(ref, ref, slot, k_peer(1))

    others = pl.ds(1, n - 1)
    body = pl.ds(0, n * LANES)
    seven = pl.ds(0, n - 1)
    seven_tiles = pl.ds(0, (n - 1) * LANES)
    seven_chunks = pl.ds(0, (n - 1) * chunk)

    mine = tile(y)
    last = pl.ds(n * LANES, LANES)
    here = cols(k * chunk, chunk)
    my_rows = pl.ds(pl.multiple_of(y * n, n), n)

    def extra_cols(yy):
        return tile(chunk_of_extra(yy) * per_chunk + n)

    bounds = [(sum(splits[:s]), splits[s]) for s in range(len(splits))]
    own = []
    for s, (first, count) in enumerate(bounds):
        c = pltpu.make_async_copy(
            grad_ref.at[:, cols(k * chunk + first * LANES, count * LANES)],
            parts.at[0, :, pl.ds(first * LANES, count * LANES)],
            local_sem.at[s],
        )
        c.start()
        own.append(c)
    own_extra = pltpu.make_async_copy(
        grad_ref.at[:, extra_cols(y)], extra_parts.at[0], local_sem.at[len(splits) + 2]
    )
    own_extra.start()
    own_master = pltpu.make_async_copy(master_ref.at[:, here], master_rows.at[k], local_sem.at[len(splits)])
    own_master.start()
    own_state = pltpu.make_async_copy(col_state_ref, col_state, local_sem.at[len(splits) + 1])
    own_state.start()

    barrier = pltpu.get_barrier_semaphore()
    peers = [k_peer(d) for d in range(1, n)] + [y_peer(d) for d in range(1, n)] + [m_peer(d) for d in range(1, nm)]
    for device in peers:
        pl.semaphore_signal(barrier, inc=1, device_id=device, device_id_type=MESH)
    pl.semaphore_wait(barrier, len(peers))

    def part_group(first, count):
        return start_all(
            parts.at[others, :, pl.ds(first * LANES, count * LANES)],
            lambda slot, d: remote(
                grad_ref.at[:, cols(k_of(d) * chunk + first * LANES, count * LANES)],
                parts.at[d, :, pl.ds(first * LANES, count * LANES)],
                slot,
                k_peer(d),
            ),
        )

    mrow = start_all(
        master_rows.at[seven],
        lambda slot, d: remote(master_ref.at[:, cols(k_of(d) * chunk, chunk)], master_rows.at[k], slot, k_peer(d))
    )
    part = [part_group(*bounds[0])]
    extra_group = start_all(
        extra_parts.at[others],
        lambda slot, d: remote(grad_ref.at[:, extra_cols(y_of(d))], extra_parts.at[d], slot, y_peer(d)),
    )
    part += [part_group(*b) for b in bounds[1:]]
    own_master.wait()
    mrow.wait_recv()
    master_full[my_rows, :] = jnp.concatenate([master_rows[r] for r in range(n)], axis=0)
    m_slot, mp_slot, mx_slot = slots.take(), slots.take(), slots.take()

    def master_copy(where, slot, device):
        part = master_full.at[my_rows, where]
        return remote(part, part, slot, device)

    @pl.when(jnp.logical_not(lower))
    def _():
        for d in range(1, n):
            master_copy(body, m_slot, y_peer(d)).start()

    @pl.when(lower)
    def _():
        for d in range(1, n):
            master_copy(tile(y_of(d)), mp_slot, y_peer(d)).start()

    @pl.when(jnp.logical_not(is_heavy))
    def _():
        master_copy(last, mx_slot, y_dev(lax.rem(k + shift, n))).start()

    def master_whole(count, where, slot):
        return whole_of(master_full.at[pl.ds(0, count * n), where], slot)

    tile_slot = slots.take()
    extra_slot = slots.take()
    tiles_in = remote(tile_in.at[others], tile_in.at[others], tile_slot, k_peer(1))
    extras_whole = extra_in.at[pl.ds(0, 2 * (n - 1))]
    extras_in = remote(extra_in.at[others], extra_in.at[others], extra_slot, k_peer(1))

    def tile_copy(d, t):
        return remote(chunk_sum.at[:, tile(t)], tile_in.at[d], tile_slot, y_peer(d))

    def extra_copy(d):
        return remote(extra_sum, extra_in.at[d], extra_slot, k_peer(d))

    for s, (first, count) in enumerate(bounds):
        where = pl.ds(first * LANES, count * LANES)
        own[s].wait()
        part[s].wait_recv()
        total = parts[0, :, where].astype(F32)
        for d in range(1, n):
            total = total + parts[d, :, where].astype(F32)
        chunk_sum[:, where] = total
        for t in range(first, first + count):

            @pl.when(y != t)
            def _():
                tile_copy(lax.rem(t - y + n, n), t).start()

        if s == 0:
            own_extra.wait()
            extra_group.wait_recv()
            total = extra_parts[0].astype(F32)
            for d in range(1, n):
                total = total + extra_parts[d].astype(F32)
            extra_sum[...] = total

            @pl.when(jnp.logical_not(is_heavy))
            def _():
                extra_copy(heavy_at).start()

    @pl.when(jnp.logical_not(is_heavy))
    def _():
        extra_in[0] = jnp.zeros((rows, LANES), F32)

    tiles_in.wait_recv()
    gradient = chunk_sum[:, mine]
    for d in range(1, n):
        gradient = gradient + tile_in[d]

    @pl.when(is_heavy)
    def _():
        extras_in.wait_recv()
        more = extra_sum[...]
        for d in range(1, n):
            more = more + extra_in[d]
        extra_in[0] = more

    gradient_x = extra_in[0]

    own_state.wait()
    square = gradient * gradient
    square_x = gradient_x * gradient_x

    def new_col(sq, t):
        state = col_state[:, tile(k * per_chunk + t)]
        total = jnp.sum(sq, axis=0, keepdims=True)
        return decay_rate * state + (1.0 - decay_rate) * (total / rows + tiny_term)

    col_new = new_col(square, y)
    col_new_x = new_col(square_x, n)
    half = gradient * lax.rsqrt(col_new)
    half_x = gradient_x * lax.rsqrt(col_new_x)
    both = jnp.concatenate([square + square_x, half * half + half_x * half_x], axis=0)
    sums = lax.dot_general(
        jnp.ones((8, LANES), F32),
        both,
        (((1,), (1,)), ((), ())),
        precision=lax.Precision.HIGHEST,
        preferred_element_type=F32,
    )

    def exchange(stage, members, peer, value):
        stat[stage, 0] = value
        slot = slots.take()
        for d in range(1, members):
            remote(stat.at[stage, 0], stat.at[stage, d], slot, peer(d)).start()
        if members == 1:
            return None
        whole = stat.at[stage, pl.ds(1, members - 1)]
        group = remote(whole, whole, slot, k_peer(1))
        sent.append(group)
        return group

    def collect(stage, members, group, value):
        if group is not None:
            group.wait_recv()
        for d in range(1, members):
            value = value + stat[stage, d]
        return value

    lane = lax.broadcasted_iota(jnp.int32, sums.shape, 1)
    line = lax.broadcasted_iota(jnp.int32, sums.shape, 0)
    state = jnp.where((lane == dp) & (m == 0), jnp.broadcast_to(row_state_ref[...], sums.shape), 0.0)
    sums = jnp.where(line == 1, state, sums)
    stat_group = exchange(0, n, y_peer, sums)

    half_full[:, mine] = half
    half_last = half_full.at[my_rows, last]
    h_slot, hl_slot, hx_slot = slots.take(), slots.take(), slots.take()

    def half_copy(count, slot, d):
        part = half_full.at[pl.ds(0, count), mine]
        return remote(part, part, slot, y_peer(d))

    def half_whole(tiles, count, slot):
        return whole_of(half_full.at[pl.ds(0, count), pl.ds(0, tiles * LANES)], slot)

    @pl.when(is_heavy)
    def _():
        half_full[:, last] = half_x

    col_chunk[:, mine] = col_new
    ccopy = start_all(
        col_chunk.at[:, seven_tiles],
        lambda slot, d: remote(col_chunk.at[:, mine], col_chunk.at[:, mine], slot, y_peer(d)),
    )
    col_last = col_chunk.at[:, last]
    cx_slot = slots.take()

    @pl.when(is_heavy)
    def _():
        col_chunk[:, last] = col_new_x
        for d in range(1, n):
            remote(col_last, col_last, cx_slot, y_peer(d)).start()

    @pl.when(jnp.logical_not(lower))
    def _():
        master_whole(y_top - 1, body, m_slot).wait_recv()
        master_whole(n - y_top, last, mp_slot).wait_recv()

    @pl.when(lower)
    def _():
        master_whole(y_top, body, m_slot).wait_recv()
        if n - y_top > 1:
            master_whole(n - y_top - 1, last, mp_slot).wait_recv()

    @pl.when(is_heavy)
    def _():
        master_whole(n - 1, last, mx_slot).wait_recv()

    side_tile[0] = half[top:, :]
    side_tile[1] = master_full[top:, mine]
    scopy = start_all(side.at[seven], lambda slot, d: remote(side_tile, side.at[k], slot, k_peer(d)))
    side[k] = side_tile[...]
    sx_slot = slots.take()

    @pl.when(is_heavy)
    def _():
        side_extra[0] = half_x
        side_extra[1] = master_full[:, last]
        for d in range(1, n):
            remote(side_extra, side_extra, sx_slot, k_peer(d)).start()

    sums = collect(0, n, stat_group, sums)
    stat_group = exchange(1, nm, m_peer, sums)
    for d in range(1, n):

        @pl.when(y_of(d) < y_top)
        def _():
            half_copy(top, h_slot, d).start()

        @pl.when(y_of(d) >= y_top)
        def _():
            half_copy(rows, hl_slot, d).start()

    @pl.when(is_heavy)
    def _():
        for d in range(1, n):
            part = half_full.at[pl.ds(pl.multiple_of(y_of(d) * n, n), n), last]
            remote(part, part, hx_slot, y_peer(d)).start()

    ccopy.wait_recv()

    @pl.when(jnp.logical_not(is_heavy))
    def _():
        remote(col_last, col_last, cx_slot, y_peer(1)).wait_recv()

    ocopy = start_all(
        col_out.at[:, seven_chunks],
        lambda slot, d: remote(col_chunk, col_out.at[:, here], slot, k_peer(d)),
    )
    col_out[:, here] = col_chunk[...]
    sums = collect(1, nm, stat_group, sums)
    stat_group = exchange(2, n, k_peer, sums)

    @pl.when(jnp.logical_not(lower))
    def _():
        half_whole(n - 1, top, h_slot).wait_recv()

    @pl.when(lower)
    def _():
        half_whole(n - 1, rows, hl_slot).wait_recv()

    scopy.wait_recv()

    @pl.when(jnp.logical_not(is_heavy))
    def _():
        remote(half_last, half_last, hx_slot, y_peer(1)).wait_recv()
        remote(side_extra, side_extra, sx_slot, k_peer(1)).wait_recv()

    sums = collect(2, n, stat_group, sums)

    row_total = sums[0:1, :rows]
    update_total = sums[0:1, rows:]
    row_state = sums[1:2, :rows]
    row_new = decay_rate * row_state + (1.0 - decay_rate) * (row_total / ff + tiny_term)
    mean_row = jnp.sum(row_new, axis=1, keepdims=True) / rows
    energy = mean_row * jnp.sum(update_total / row_new, axis=1, keepdims=True)
    scale = jnp.maximum(1.0, jnp.sqrt(energy / (rows * ff)) / clip_level)
    factor = lax.rsqrt(row_new) * (step_size * jnp.sqrt(mean_row) / scale)
    eye = lax.broadcasted_iota(jnp.int32, (rows, rows), 0) == lax.broadcasted_iota(jnp.int32, (rows, rows), 1)
    factor = jnp.sum(jnp.where(eye, jnp.broadcast_to(factor, (rows, rows)), 0.0), axis=1, keepdims=True)

    for first, count in bounds:
        where = pl.ds(first * LANES, count * LANES)
        fresh = master_full[:top, where] - factor[:top] * half_full[:top, where]
        weight_out[:top, cols(k * chunk + first * LANES, count * LANES)] = fresh.astype(BF16)
    upper = weight_out.at[pl.ds(0, top), cols(k * chunk, n * LANES)]
    wcopy = start_all(weight_out.at[pl.ds(0, top), pl.ds(0, (n - 1) * n * LANES)], lambda slot, d: remote(upper, upper, slot, k_peer(d)))

    weight_out[:, extra_cols(y)] = (side_extra[1] - factor * side_extra[0]).astype(BF16)
    extra_out = weight_out.at[:, extra_cols(y)]
    xcopy = start_all(weight_out.at[:, seven_tiles], lambda slot, d: remote(extra_out, extra_out, slot, y_peer(d)))

    def side_tile_at(j, yy):
        return tile(j * per_chunk + yy)

    for j in range(n):
        fresh = (side[j, 1] - factor[top:] * side[j, 0]).astype(BF16)
        side_send[:, pl.ds(j * LANES, LANES)] = fresh
        weight_out[top:, side_tile_at(j, y)] = fresh
    ucopy = start_all(side_in.at[others], lambda slot, d: remote(side_send, side_in.at[d], slot, y_peer(d)))

    pick = lax.broadcasted_iota(jnp.int32, (n, rows), 1) - y * n == lax.broadcasted_iota(jnp.int32, (n, rows), 0)
    row_factor = lax.rsqrt(row_new) * (step_size * jnp.sqrt(mean_row) / scale)
    row_factor = jnp.sum(jnp.where(pick, jnp.broadcast_to(row_factor, (n, rows)), 0.0), axis=1, keepdims=True)
    fresh = master_full[my_rows, :] - row_factor * half_full[my_rows, :]
    for r in range(n):
        fresh_rows[r] = fresh[r : r + 1, :]
    fcopy = start_all(master_out.at[:, seven_chunks], lambda slot, d: remote(fresh_rows.at[k_of(d)], master_out.at[:, here], slot, k_peer(d)))
    master_out[:, here] = fresh_rows[k]

    full_lane = lax.broadcasted_iota(jnp.int32, row_new.shape, 1)
    row_out[...] = jnp.sum(jnp.where(full_lane == dp, row_new, 0.0), axis=1, keepdims=True)

    ucopy.wait_recv()
    for d in range(1, n):
        yy = lax.rem(y - d + n, n)
        for j in range(n):
            weight_out[top:, side_tile_at(j, yy)] = side_in[d, :, pl.ds(j * LANES, LANES)]
    ocopy.wait_recv()
    fcopy.wait_recv()
    xcopy.wait_recv()
    wcopy.wait_recv()

    for group in sent:
        group.wait_send()
    tiles_in.wait_send()

    @pl.when(jnp.logical_not(lower))
    def _():
        master_whole(n - 1, body, m_slot).wait_send()
        half_whole(y_top - 1, top, h_slot).wait_send()
        half_whole(n - y_top, rows, hl_slot).wait_send()

    @pl.when(lower)
    def _():
        master_whole(n - 1, last, mp_slot).wait_send()
        half_whole(y_top, top, h_slot).wait_send()
        if n - y_top > 1:
            half_whole(n - y_top - 1, rows, hl_slot).wait_send()

    @pl.when(jnp.logical_not(is_heavy))
    def _():
        master_copy(last, mx_slot, y_peer(1)).wait_send()

    @pl.when(jnp.logical_not(is_heavy))
    def _():
        extra_copy(heavy_at).wait_send()

    @pl.when(is_heavy)
    def _():
        whole_of(half_full.at[pl.ds(0, n), seven_tiles], hx_slot).wait_send()
        remote(col_chunk.at[:, seven_tiles], col_chunk.at[:, seven_tiles], cx_slot, y_peer(1)).wait_send()
        remote(extras_whole, extras_whole, sx_slot, k_peer(1)).wait_send()


def writer(*refs):
    *pairs, sem = refs
    count = len(pairs) // 2
    copies = [pltpu.make_async_copy(pairs[i], pairs[count + i], sem.at[i]) for i in range(count)]
    for c in copies:
        c.start()
    for c in copies:
        c.wait()


def build(n, nm, splits):
    def per_device(grad_partials, master, row_state, col_state):
        grad = grad_partials[0]
        rows, width = grad.shape
        chunk = width // n
        quarter = rows // 4
        hbm = pl.BlockSpec(memory_space=pltpu.HBM)
        vmem = pl.BlockSpec(memory_space=pltpu.VMEM)
        dma = pltpu.SemaphoreType.DMA

        def in_hbm(a):
            return pltpu.with_memory_space_constraint(a, pltpu.HBM)

        out = pl.pallas_call(
            functools.partial(kernel, n, nm, splits),
            out_shape=(
                jax.ShapeDtypeStruct((1, width), F32),
                jax.ShapeDtypeStruct((rows, width), BF16),
                jax.ShapeDtypeStruct((1, 1), F32),
                jax.ShapeDtypeStruct((1, width), F32),
            ),
            in_specs=[hbm, hbm, vmem, hbm],
            out_specs=(vmem, vmem, vmem, vmem),
            scratch_shapes=[
                pltpu.VMEM((n, rows, chunk), BF16),
                pltpu.VMEM((rows, chunk), F32),
                pltpu.VMEM((n, rows, LANES), F32),
                pltpu.VMEM((n, rows, LANES), BF16),
                pltpu.VMEM((rows, LANES), F32),
                pltpu.VMEM((2 * n, rows, LANES), F32),
                pltpu.VMEM((n, 1, chunk), F32),
                pltpu.VMEM((rows, chunk), F32),
                pltpu.VMEM((rows, chunk), F32),
                pltpu.VMEM((2, quarter, LANES), F32),
                pltpu.VMEM((2, rows, LANES), F32),
                pltpu.VMEM((n, 2, quarter, LANES), F32),
                pltpu.VMEM((quarter, n * LANES), BF16),
                pltpu.VMEM((n, quarter, n * LANES), BF16),
                pltpu.VMEM((3, max(n, nm), 8, 2 * rows), F32),
                pltpu.VMEM((n, 1, chunk), F32),
                pltpu.VMEM((1, chunk), F32),
                pltpu.VMEM((1, width), F32),
                dma((len(splits) + 3,)),
                dma((28,)),
                dma((28,)),
            ],
            compiler_params=pltpu.CompilerParams(
                collective_id=0, has_side_effects=True, vmem_limit_bytes=32 * 1024 * 1024
            ),
        )(in_hbm(grad), in_hbm(master), row_state.reshape(1, 1), in_hbm(col_state.reshape(1, width)))
        master_new, weight_full, row_new, col_new = pl.pallas_call(
            writer,
            out_shape=tuple(jax.ShapeDtypeStruct(a.shape, a.dtype) for a in out),
            in_specs=[pl.BlockSpec(memory_space=pl.ANY)] * len(out),
            out_specs=tuple([hbm] * len(out)),
            scratch_shapes=[dma((len(out),))],
            compiler_params=pltpu.CompilerParams(vmem_limit_bytes=1024 * 1024),
        )(*out)
        return (master_new, weight_full, row_new.reshape(1), col_new.reshape(width))

    return per_device


def solution(mesh):
    in_specs = (P("dp", None, "mp"), P("dp", "mp"), P("dp"), P("mp"))
    out_specs = (P("dp", "mp"), P(None, "mp"), P("dp"), P("mp"))
    return jax.shard_map(
        build(8, 8, (3, 3, 2)), mesh=mesh, in_specs=in_specs, out_specs=out_specs, check_vma=False
    )
```

```python
import functools

import jax
import jax.numpy as jnp
from jax import lax
from jax.experimental import pallas as pl
from jax.experimental.pallas import tpu as pltpu
from jax.sharding import PartitionSpec as P

MESH = pl.DeviceIdType.MESH
LANES = 128
F32, BF16 = jnp.float32, jnp.bfloat16

decay_rate = 0.5
clip_level = 1.0
step_size = 0.5
tiny_term = 1e-30


class Slots:
    def __init__(self):
        self.used = 0

    def take(self, n=1):
        self.used += n
        return self.used - n


def kernel(
    n,
    nm,
    splits,
    grad_ref,
    master_ref,
    row_state_ref,
    col_state_ref,
    master_out,
    weight_out,
    row_out,
    col_out,
    parts,
    chunk_sum,
    tile_in,
    extra_parts,
    extra_sum,
    extra_in,
    master_rows,
    master_full,
    half_full,
    side_tile,
    side_extra,
    side,
    side_send,
    side_in,
    stat,
    fresh_rows,
    col_chunk,
    col_state,
    local_sem,
    send_sem,
    recv_sem,
):
    rows, chunk = chunk_sum.shape
    ff = chunk * n * nm
    per_chunk = n + 1
    q = side_in.shape[1]
    top = rows - q

    dp = lax.axis_index("dp")
    m = lax.axis_index("mp")
    y = dp // n
    k = lax.rem(dp, n)
    shift = (n // 2) * lax.rem(m, 2)
    is_heavy = lax.rem(k + shift, n) == y

    def chunk_of_extra(yy):
        return lax.rem(yy + shift, n)

    y_top = top // n
    lower = y >= y_top
    heavy_at = lax.rem(chunk_of_extra(y) - k + n, n)

    def k_of(d):
        return lax.rem(k + d, n)

    def y_of(d):
        return lax.rem(y + d, n)

    def k_peer(d):
        return (y * n + k_of(d), m)

    def y_dev(yy):
        return (yy * n + k, m)

    def y_peer(d):
        return y_dev(y_of(d))

    def m_peer(d):
        return (dp, lax.rem(m + d, nm))

    def cols(start, width):
        return pl.ds(pl.multiple_of(start, LANES), width)

    def tile(t):
        return cols(t * LANES, LANES)

    slots = Slots()
    sent = []

    def remote(src, dst, slot, device):
        return pltpu.make_async_remote_copy(
            src_ref=src,
            dst_ref=dst,
            send_sem=send_sem.at[slot],
            recv_sem=recv_sem.at[slot],
            device_id=device,
            device_id_type=MESH,
        )

    def start_all(whole, make):
        slot = slots.take()
        for d in range(1, n):
            make(slot, d).start()
        group = remote(whole, whole, slot, k_peer(1))
        sent.append(group)
        return group

    def whole_of(ref, slot):
        return remote(ref, ref, slot, k_peer(1))

    others = pl.ds(1, n - 1)
    body = pl.ds(0, n * LANES)
    seven = pl.ds(0, n - 1)
    seven_tiles = pl.ds(0, (n - 1) * LANES)
    seven_chunks = pl.ds(0, (n - 1) * chunk)

    mine = tile(y)
    last = pl.ds(n * LANES, LANES)
    here = cols(k * chunk, chunk)
    my_rows = pl.ds(pl.multiple_of(y * n, n), n)

    barrier = pltpu.get_barrier_semaphore()
    peers = [k_peer(d) for d in range(1, n)] + [y_peer(d) for d in range(1, n)] + [m_peer(d) for d in range(1, nm)]
    for device in peers:
        pl.semaphore_signal(barrier, inc=1, device_id=device, device_id_type=MESH)

    def extra_cols(yy):
        return tile(chunk_of_extra(yy) * per_chunk + n)

    bounds = [(sum(splits[:s]), splits[s]) for s in range(len(splits))]
    own = []
    for s, (first, count) in enumerate(bounds):
        c = pltpu.make_async_copy(
            grad_ref.at[:, cols(k * chunk + first * LANES, count * LANES)],
            parts.at[0, :, pl.ds(first * LANES, count * LANES)],
            local_sem.at[s],
        )
        c.start()
        own.append(c)
    own_extra = pltpu.make_async_copy(
        grad_ref.at[:, extra_cols(y)], extra_parts.at[0], local_sem.at[len(splits) + 2]
    )
    own_extra.start()
    own_master = pltpu.make_async_copy(master_ref.at[:, here], master_rows.at[k], local_sem.at[len(splits)])
    own_master.start()
    own_state = pltpu.make_async_copy(col_state_ref, col_state, local_sem.at[len(splits) + 1])
    own_state.start()

    pl.semaphore_wait(barrier, len(peers))

    def part_group(first, count):
        return start_all(
            parts.at[others, :, pl.ds(first * LANES, count * LANES)],
            lambda slot, d: remote(
                grad_ref.at[:, cols(k_of(d) * chunk + first * LANES, count * LANES)],
                parts.at[d, :, pl.ds(first * LANES, count * LANES)],
                slot,
                k_peer(d),
            ),
        )

    mrow = start_all(
        master_rows.at[seven],
        lambda slot, d: remote(master_ref.at[:, cols(k_of(d) * chunk, chunk)], master_rows.at[k], slot, k_peer(d))
    )
    part = [part_group(*bounds[0])]
    extra_group = start_all(
        extra_parts.at[others],
        lambda slot, d: remote(grad_ref.at[:, extra_cols(y_of(d))], extra_parts.at[d], slot, y_peer(d)),
    )
    part += [part_group(*b) for b in bounds[1:]]
    own_master.wait()
    mrow.wait_recv()
    master_full[my_rows, :] = jnp.concatenate([master_rows[r] for r in range(n)], axis=0)
    m_slot, mp_slot, mx_slot = slots.take(), slots.take(), slots.take()

    def master_copy(where, slot, device):
        part = master_full.at[my_rows, where]
        return remote(part, part, slot, device)

    @pl.when(jnp.logical_not(lower))
    def _():
        for d in range(1, n):
            master_copy(body, m_slot, y_peer(d)).start()

    @pl.when(lower)
    def _():
        for d in range(1, n):
            master_copy(tile(y_of(d)), mp_slot, y_peer(d)).start()

    @pl.when(jnp.logical_not(is_heavy))
    def _():
        master_copy(last, mx_slot, y_dev(lax.rem(k + shift, n))).start()

    def master_whole(count, where, slot):
        return whole_of(master_full.at[pl.ds(0, count * n), where], slot)

    tile_slot = slots.take()
    extra_slot = slots.take()
    tiles_in = remote(tile_in.at[others], tile_in.at[others], tile_slot, k_peer(1))
    extras_whole = extra_in.at[pl.ds(0, 2 * (n - 1))]
    extras_in = remote(extra_in.at[others], extra_in.at[others], extra_slot, k_peer(1))

    def tile_copy(d, t):
        return remote(chunk_sum.at[:, tile(t)], tile_in.at[d], tile_slot, y_peer(d))

    def extra_copy(d):
        return remote(extra_sum, extra_in.at[d], extra_slot, k_peer(d))

    for s, (first, count) in enumerate(bounds):
        where = pl.ds(first * LANES, count * LANES)
        own[s].wait()
        part[s].wait_recv()
        total = parts[0, :, where].astype(F32)
        for d in range(1, n):
            total = total + parts[d, :, where].astype(F32)
        chunk_sum[:, where] = total
        for t in range(first, first + count):

            @pl.when(y != t)
            def _():
                tile_copy(lax.rem(t - y + n, n), t).start()

        if s == 0:
            own_extra.wait()
            extra_group.wait_recv()
            total = extra_parts[0].astype(F32)
            for d in range(1, n):
                total = total + extra_parts[d].astype(F32)
            extra_sum[...] = total

            @pl.when(jnp.logical_not(is_heavy))
            def _():
                extra_copy(heavy_at).start()

    @pl.when(jnp.logical_not(is_heavy))
    def _():
        extra_in[0] = jnp.zeros((rows, LANES), F32)

    tiles_in.wait_recv()
    gradient = chunk_sum[:, mine]
    for d in range(1, n):
        gradient = gradient + tile_in[d]

    @pl.when(is_heavy)
    def _():
        extras_in.wait_recv()
        more = extra_sum[...]
        for d in range(1, n):
            more = more + extra_in[d]
        extra_in[0] = more

    gradient_x = extra_in[0]

    own_state.wait()
    square = gradient * gradient
    square_x = gradient_x * gradient_x

    def new_col(sq, t):
        state = col_state[:, tile(k * per_chunk + t)]
        total = jnp.sum(sq, axis=0, keepdims=True)
        return decay_rate * state + (1.0 - decay_rate) * (total / rows + tiny_term)

    col_new = new_col(square, y)
    col_new_x = new_col(square_x, n)
    half = gradient * lax.rsqrt(col_new)
    half_x = gradient_x * lax.rsqrt(col_new_x)
    both = jnp.concatenate([square + square_x, half * half + half_x * half_x], axis=0)
    sums = lax.dot_general(
        jnp.ones((8, LANES), F32),
        both,
        (((1,), (1,)), ((), ())),
        precision=lax.Precision.HIGHEST,
        preferred_element_type=F32,
    )

    def exchange(stage, members, peer, value):
        stat[stage, 0] = value
        slot = slots.take()
        for d in range(1, members):
            remote(stat.at[stage, 0], stat.at[stage, d], slot, peer(d)).start()
        if members == 1:
            return None
        whole = stat.at[stage, pl.ds(1, members - 1)]
        group = remote(whole, whole, slot, k_peer(1))
        sent.append(group)
        return group

    def collect(stage, members, group, value):
        if group is not None:
            group.wait_recv()
        for d in range(1, members):
            value = value + stat[stage, d]
        return value

    lane = lax.broadcasted_iota(jnp.int32, sums.shape, 1)
    line = lax.broadcasted_iota(jnp.int32, sums.shape, 0)
    state = jnp.where((lane == dp) & (m == 0), jnp.broadcast_to(row_state_ref[...], sums.shape), 0.0)
    sums = jnp.where(line == 1, state, sums)
    stat_group = exchange(0, n, y_peer, sums)

    half_full[:, mine] = half
    half_last = half_full.at[my_rows, last]
    h_slot, hl_slot, hx_slot = slots.take(), slots.take(), slots.take()

    def half_copy(count, slot, d):
        part = half_full.at[pl.ds(0, count), mine]
        return remote(part, part, slot, y_peer(d))

    def half_whole(tiles, count, slot):
        return whole_of(half_full.at[pl.ds(0, count), pl.ds(0, tiles * LANES)], slot)

    @pl.when(is_heavy)
    def _():
        half_full[:, last] = half_x

    for d in (1, 7):

        @pl.when(y_of(d) < y_top)
        def _():
            half_copy(top, h_slot, d).start()

        @pl.when(y_of(d) >= y_top)
        def _():
            half_copy(rows, hl_slot, d).start()

    col_chunk[:, mine] = col_new
    ccopy = start_all(
        col_chunk.at[:, seven_tiles],
        lambda slot, d: remote(col_chunk.at[:, mine], col_chunk.at[:, mine], slot, y_peer(d)),
    )
    col_last = col_chunk.at[:, last]
    cx_slot = slots.take()

    @pl.when(is_heavy)
    def _():
        col_chunk[:, last] = col_new_x
        for d in range(1, n):
            remote(col_last, col_last, cx_slot, y_peer(d)).start()

    @pl.when(jnp.logical_not(lower))
    def _():
        master_whole(y_top - 1, body, m_slot).wait_recv()
        master_whole(n - y_top, last, mp_slot).wait_recv()

    @pl.when(lower)
    def _():
        master_whole(y_top, body, m_slot).wait_recv()
        if n - y_top > 1:
            master_whole(n - y_top - 1, last, mp_slot).wait_recv()

    @pl.when(is_heavy)
    def _():
        master_whole(n - 1, last, mx_slot).wait_recv()

    side_tile[0] = half[top:, :]
    side_tile[1] = master_full[top:, mine]
    scopy = start_all(side.at[seven], lambda slot, d: remote(side_tile, side.at[k], slot, k_peer(d)))
    side[k] = side_tile[...]
    sx_slot = slots.take()

    @pl.when(is_heavy)
    def _():
        side_extra[0] = half_x
        side_extra[1] = master_full[:, last]
        for d in range(1, n):
            remote(side_extra, side_extra, sx_slot, k_peer(d)).start()

    sums = collect(0, n, stat_group, sums)
    stat_group = exchange(1, nm, m_peer, sums)
    for d in (4, 3, 5, 2, 6):

        @pl.when(y_of(d) < y_top)
        def _():
            half_copy(top, h_slot, d).start()

        @pl.when(y_of(d) >= y_top)
        def _():
            half_copy(rows, hl_slot, d).start()

    @pl.when(is_heavy)
    def _():
        for d in range(1, n):
            part = half_full.at[pl.ds(pl.multiple_of(y_of(d) * n, n), n), last]
            remote(part, part, hx_slot, y_peer(d)).start()

    ccopy.wait_recv()

    @pl.when(jnp.logical_not(is_heavy))
    def _():
        remote(col_last, col_last, cx_slot, y_peer(1)).wait_recv()

    ocopy = start_all(
        col_out.at[:, seven_chunks],
        lambda slot, d: remote(col_chunk, col_out.at[:, here], slot, k_peer(d)),
    )
    col_out[:, here] = col_chunk[...]
    sums = collect(1, nm, stat_group, sums)
    stat_group = exchange(2, n, k_peer, sums)

    @pl.when(jnp.logical_not(lower))
    def _():
        half_whole(n - 1, top, h_slot).wait_recv()

    @pl.when(lower)
    def _():
        half_whole(n - 1, rows, hl_slot).wait_recv()

    scopy.wait_recv()

    @pl.when(jnp.logical_not(is_heavy))
    def _():
        remote(half_last, half_last, hx_slot, y_peer(1)).wait_recv()
        remote(side_extra, side_extra, sx_slot, k_peer(1)).wait_recv()

    sums = collect(2, n, stat_group, sums)

    row_total = sums[0:1, :rows]
    update_total = sums[0:1, rows:]
    row_state = sums[1:2, :rows]
    row_new = decay_rate * row_state + (1.0 - decay_rate) * (row_total / ff + tiny_term)
    mean_row = jnp.sum(row_new, axis=1, keepdims=True) / rows
    energy = mean_row * jnp.sum(update_total / row_new, axis=1, keepdims=True)
    scale = jnp.maximum(1.0, jnp.sqrt(energy / (rows * ff)) / clip_level)
    factor = lax.rsqrt(row_new) * (step_size * jnp.sqrt(mean_row) / scale)
    eye = lax.broadcasted_iota(jnp.int32, (rows, rows), 0) == lax.broadcasted_iota(jnp.int32, (rows, rows), 1)
    factor = jnp.sum(jnp.where(eye, jnp.broadcast_to(factor, (rows, rows)), 0.0), axis=1, keepdims=True)

    for first, count in bounds:
        where = pl.ds(first * LANES, count * LANES)
        fresh = master_full[:top, where] - factor[:top] * half_full[:top, where]
        weight_out[:top, cols(k * chunk + first * LANES, count * LANES)] = fresh.astype(BF16)
    upper = weight_out.at[pl.ds(0, top), cols(k * chunk, n * LANES)]
    wcopy = start_all(weight_out.at[pl.ds(0, top), pl.ds(0, (n - 1) * n * LANES)], lambda slot, d: remote(upper, upper, slot, k_peer(d)))

    weight_out[:, extra_cols(y)] = (side_extra[1] - factor * side_extra[0]).astype(BF16)
    extra_out = weight_out.at[:, extra_cols(y)]
    xcopy = start_all(weight_out.at[:, seven_tiles], lambda slot, d: remote(extra_out, extra_out, slot, y_peer(d)))

    def side_tile_at(j, yy):
        return tile(j * per_chunk + yy)

    for j in range(n):
        fresh = (side[j, 1] - factor[top:] * side[j, 0]).astype(BF16)
        side_send[:, pl.ds(j * LANES, LANES)] = fresh
        weight_out[top:, side_tile_at(j, y)] = fresh
    ucopy = start_all(side_in.at[others], lambda slot, d: remote(side_send, side_in.at[d], slot, y_peer(d)))

    pick = lax.broadcasted_iota(jnp.int32, (n, rows), 1) - y * n == lax.broadcasted_iota(jnp.int32, (n, rows), 0)
    row_factor = lax.rsqrt(row_new) * (step_size * jnp.sqrt(mean_row) / scale)
    row_factor = jnp.sum(jnp.where(pick, jnp.broadcast_to(row_factor, (n, rows)), 0.0), axis=1, keepdims=True)
    fresh = master_full[my_rows, :] - row_factor * half_full[my_rows, :]
    for r in range(n):
        fresh_rows[r] = fresh[r : r + 1, :]
    fcopy = start_all(master_out.at[:, seven_chunks], lambda slot, d: remote(fresh_rows.at[k_of(d)], master_out.at[:, here], slot, k_peer(d)))
    master_out[:, here] = fresh_rows[k]

    full_lane = lax.broadcasted_iota(jnp.int32, row_new.shape, 1)
    row_out[...] = jnp.sum(jnp.where(full_lane == dp, row_new, 0.0), axis=1, keepdims=True)

    ucopy.wait_recv()
    for d in range(1, n):
        yy = lax.rem(y - d + n, n)
        for j in range(n):
            weight_out[top:, side_tile_at(j, yy)] = side_in[d, :, pl.ds(j * LANES, LANES)]
    ocopy.wait_recv()
    fcopy.wait_recv()
    xcopy.wait_recv()
    wcopy.wait_recv()

    for group in sent:
        group.wait_send()
    tiles_in.wait_send()

    @pl.when(jnp.logical_not(lower))
    def _():
        master_whole(n - 1, body, m_slot).wait_send()
        half_whole(y_top - 1, top, h_slot).wait_send()
        half_whole(n - y_top, rows, hl_slot).wait_send()

    @pl.when(lower)
    def _():
        master_whole(n - 1, last, mp_slot).wait_send()
        half_whole(y_top, top, h_slot).wait_send()
        if n - y_top > 1:
            half_whole(n - y_top - 1, rows, hl_slot).wait_send()

    @pl.when(jnp.logical_not(is_heavy))
    def _():
        master_copy(last, mx_slot, y_peer(1)).wait_send()

    @pl.when(jnp.logical_not(is_heavy))
    def _():
        extra_copy(heavy_at).wait_send()

    @pl.when(is_heavy)
    def _():
        whole_of(half_full.at[pl.ds(0, n), seven_tiles], hx_slot).wait_send()
        remote(col_chunk.at[:, seven_tiles], col_chunk.at[:, seven_tiles], cx_slot, y_peer(1)).wait_send()
        remote(extras_whole, extras_whole, sx_slot, k_peer(1)).wait_send()


def writer(*refs):
    *pairs, sem = refs
    count = len(pairs) // 2
    copies = []
    for a, b in zip(pairs[:count], pairs[count:]):
        step = min(a.shape[0], 16)
        for r in range(0, a.shape[0], step):
            piece = pl.ds(r, step)
            copies.append(pltpu.make_async_copy(a.at[piece], b.at[piece], sem.at[len(copies)]))
    for c in copies:
        c.start()
    for c in copies:
        c.wait()


def build(n, nm, splits):
    def per_device(grad_partials, master, row_state, col_state):
        grad = grad_partials[0]
        rows, width = grad.shape
        chunk = width // n
        quarter = rows // 4
        hbm = pl.BlockSpec(memory_space=pltpu.HBM)
        vmem = pl.BlockSpec(memory_space=pltpu.VMEM)
        dma = pltpu.SemaphoreType.DMA

        def in_hbm(a):
            return pltpu.with_memory_space_constraint(a, pltpu.HBM)

        out = pl.pallas_call(
            functools.partial(kernel, n, nm, splits),
            out_shape=(
                jax.ShapeDtypeStruct((1, width), F32),
                jax.ShapeDtypeStruct((rows, width), BF16),
                jax.ShapeDtypeStruct((1, 1), F32),
                jax.ShapeDtypeStruct((1, width), F32),
            ),
            in_specs=[hbm, hbm, vmem, hbm],
            out_specs=(vmem, vmem, vmem, vmem),
            scratch_shapes=[
                pltpu.VMEM((n, rows, chunk), BF16),
                pltpu.VMEM((rows, chunk), F32),
                pltpu.VMEM((n, rows, LANES), F32),
                pltpu.VMEM((n, rows, LANES), BF16),
                pltpu.VMEM((rows, LANES), F32),
                pltpu.VMEM((2 * n, rows, LANES), F32),
                pltpu.VMEM((n, 1, chunk), F32),
                pltpu.VMEM((rows, chunk), F32),
                pltpu.VMEM((rows, chunk), F32),
                pltpu.VMEM((2, quarter, LANES), F32),
                pltpu.VMEM((2, rows, LANES), F32),
                pltpu.VMEM((n, 2, quarter, LANES), F32),
                pltpu.VMEM((quarter, n * LANES), BF16),
                pltpu.VMEM((n, quarter, n * LANES), BF16),
                pltpu.VMEM((3, max(n, nm), 8, 2 * rows), F32),
                pltpu.VMEM((n, 1, chunk), F32),
                pltpu.VMEM((1, chunk), F32),
                pltpu.VMEM((1, width), F32),
                dma((len(splits) + 3,)),
                dma((26,)),
                dma((26,)),
            ],
            compiler_params=pltpu.CompilerParams(
                collective_id=0, has_side_effects=True, vmem_limit_bytes=32 * 1024 * 1024
            ),
        )(in_hbm(grad), in_hbm(master), row_state.reshape(1, 1), in_hbm(col_state.reshape(1, width)))
        master_new, weight_full, row_new, col_new = pl.pallas_call(
            writer,
            out_shape=tuple(jax.ShapeDtypeStruct(a.shape, a.dtype) for a in out),
            in_specs=[pl.BlockSpec(memory_space=pl.ANY)] * len(out),
            out_specs=tuple([hbm] * len(out)),
            scratch_shapes=[dma((len(out) - 1 + -(-rows // 16),))],
            compiler_params=pltpu.CompilerParams(vmem_limit_bytes=1024 * 1024),
        )(*out)
        return (master_new, weight_full, row_new.reshape(1), col_new.reshape(width))

    return per_device


def solution(mesh):
    in_specs = (P("dp", None, "mp"), P("dp", "mp"), P("dp"), P("mp"))
    out_specs = (P("dp", "mp"), P(None, "mp"), P("dp"), P("mp"))
    return jax.shard_map(
        build(8, 8, (4, 2, 1, 1)), mesh=mesh, in_specs=in_specs, out_specs=out_specs, check_vma=False
    )
```

```python
import functools

import jax
import jax.numpy as jnp
from jax import lax
from jax.experimental import pallas as pl
from jax.experimental.pallas import tpu as pltpu
from jax.sharding import PartitionSpec as P

MESH = pl.DeviceIdType.MESH
LANES = 128
F32, BF16 = jnp.float32, jnp.bfloat16

decay_rate = 0.5
clip_level = 1.0
step_size = 0.5
tiny_term = 1e-30


class Slots:
    def __init__(self):
        self.used = 0

    def take(self, n=1):
        self.used += n
        return self.used - n


def kernel(
    n,
    nm,
    splits,
    grad_ref,
    master_ref,
    row_state_ref,
    col_state_ref,
    master_out,
    weight_out,
    row_out,
    col_out,
    parts,
    chunk_sum,
    tile_in,
    extra_parts,
    extra_sum,
    extra_in,
    master_rows,
    master_full,
    half_full,
    side_tile,
    side_extra,
    side,
    side_send,
    side_in,
    stat,
    fresh_rows,
    col_chunk,
    col_state,
    local_sem,
    send_sem,
    recv_sem,
):
    rows, chunk = chunk_sum.shape
    ff = chunk * n * nm
    per_chunk = n + 1
    q = side_in.shape[1]
    top = rows - q

    dp = lax.axis_index("dp")
    m = lax.axis_index("mp")
    y = dp // n
    k = lax.rem(dp, n)
    shift = (n // 2) * lax.rem(m, 2)
    is_heavy = lax.rem(k + shift, n) == y

    def chunk_of_extra(yy):
        return lax.rem(yy + shift, n)

    y_top = top // n
    lower = y >= y_top
    heavy_at = lax.rem(chunk_of_extra(y) - k + n, n)

    def k_of(d):
        return lax.rem(k + d, n)

    def y_of(d):
        return lax.rem(y + d, n)

    def k_peer(d):
        return (y * n + k_of(d), m)

    def y_dev(yy):
        return (yy * n + k, m)

    def y_peer(d):
        return y_dev(y_of(d))

    def m_peer(d):
        return (dp, lax.rem(m + d, nm))

    def cols(start, width):
        return pl.ds(pl.multiple_of(start, LANES), width)

    def tile(t):
        return cols(t * LANES, LANES)

    slots = Slots()
    sent = []

    def remote(src, dst, slot, device):
        return pltpu.make_async_remote_copy(
            src_ref=src,
            dst_ref=dst,
            send_sem=send_sem.at[slot],
            recv_sem=recv_sem.at[slot],
            device_id=device,
            device_id_type=MESH,
        )

    def start_all(whole, make):
        slot = slots.take()
        for d in range(1, n):
            make(slot, d).start()
        group = remote(whole, whole, slot, k_peer(1))
        sent.append(group)
        return group

    def whole_of(ref, slot):
        return remote(ref, ref, slot, k_peer(1))

    others = pl.ds(1, n - 1)
    body = pl.ds(0, n * LANES)
    seven = pl.ds(0, n - 1)
    seven_tiles = pl.ds(0, (n - 1) * LANES)
    seven_chunks = pl.ds(0, (n - 1) * chunk)

    mine = tile(y)
    last = pl.ds(n * LANES, LANES)
    here = cols(k * chunk, chunk)
    my_rows = pl.ds(pl.multiple_of(y * n, n), n)

    barrier = pltpu.get_barrier_semaphore()
    peers = [k_peer(d) for d in range(1, n)] + [y_peer(d) for d in range(1, n)] + [m_peer(d) for d in range(1, nm)]
    for device in peers:
        pl.semaphore_signal(barrier, inc=1, device_id=device, device_id_type=MESH)

    def extra_cols(yy):
        return tile(chunk_of_extra(yy) * per_chunk + n)

    bounds = [(sum(splits[:s]), splits[s]) for s in range(len(splits))]
    own = []
    for s, (first, count) in enumerate(bounds):
        c = pltpu.make_async_copy(
            grad_ref.at[:, cols(k * chunk + first * LANES, count * LANES)],
            parts.at[0, :, pl.ds(first * LANES, count * LANES)],
            local_sem.at[s],
        )
        c.start()
        own.append(c)
    own_extra = pltpu.make_async_copy(
        grad_ref.at[:, extra_cols(y)], extra_parts.at[0], local_sem.at[len(splits) + 2]
    )
    own_extra.start()
    own_master = pltpu.make_async_copy(master_ref.at[:, here], master_rows.at[k], local_sem.at[len(splits)])
    own_master.start()
    own_state = pltpu.make_async_copy(col_state_ref, col_state, local_sem.at[len(splits) + 1])
    own_state.start()

    pl.semaphore_wait(barrier, len(peers))

    def part_group(first, count):
        return start_all(
            parts.at[others, :, pl.ds(first * LANES, count * LANES)],
            lambda slot, d: remote(
                grad_ref.at[:, cols(k_of(d) * chunk + first * LANES, count * LANES)],
                parts.at[d, :, pl.ds(first * LANES, count * LANES)],
                slot,
                k_peer(d),
            ),
        )

    mrow = start_all(
        master_rows.at[seven],
        lambda slot, d: remote(master_ref.at[:, cols(k_of(d) * chunk, chunk)], master_rows.at[k], slot, k_peer(d))
    )
    part = [part_group(*bounds[0])]
    extra_group = start_all(
        extra_parts.at[others],
        lambda slot, d: remote(grad_ref.at[:, extra_cols(y_of(d))], extra_parts.at[d], slot, y_peer(d)),
    )
    part += [part_group(*b) for b in bounds[1:]]
    own_master.wait()
    mrow.wait_recv()
    master_full[my_rows, :] = jnp.concatenate([master_rows[r] for r in range(n)], axis=0)
    m_slot, mp_slot, mx_slot = slots.take(), slots.take(), slots.take()

    def master_copy(where, slot, device):
        part = master_full.at[my_rows, where]
        return remote(part, part, slot, device)

    @pl.when(jnp.logical_not(lower))
    def _():
        for d in range(1, n):
            master_copy(body, m_slot, y_peer(d)).start()

    @pl.when(lower)
    def _():
        for d in range(1, n):
            master_copy(tile(y_of(d)), mp_slot, y_peer(d)).start()

    @pl.when(jnp.logical_not(is_heavy))
    def _():
        master_copy(last, mx_slot, y_dev(lax.rem(k + shift, n))).start()

    def master_whole(count, where, slot):
        return whole_of(master_full.at[pl.ds(0, count * n), where], slot)

    tile_slot = slots.take()
    extra_slot = slots.take()
    tiles_in = remote(tile_in.at[others], tile_in.at[others], tile_slot, k_peer(1))
    extras_whole = extra_in.at[pl.ds(0, 2 * (n - 1))]
    extras_in = remote(extra_in.at[others], extra_in.at[others], extra_slot, k_peer(1))

    def tile_copy(d, t):
        return remote(chunk_sum.at[:, tile(t)], tile_in.at[d], tile_slot, y_peer(d))

    def extra_copy(d):
        return remote(extra_sum, extra_in.at[d], extra_slot, k_peer(d))

    for s, (first, count) in enumerate(bounds):
        where = pl.ds(first * LANES, count * LANES)
        own[s].wait()
        part[s].wait_recv()
        total = parts[0, :, where].astype(F32)
        for d in range(1, n):
            total = total + parts[d, :, where].astype(F32)
        chunk_sum[:, where] = total
        for t in range(first, first + count):

            @pl.when(y != t)
            def _():
                tile_copy(lax.rem(t - y + n, n), t).start()

        if s == 0:
            own_extra.wait()
            extra_group.wait_recv()
            total = extra_parts[0].astype(F32)
            for d in range(1, n):
                total = total + extra_parts[d].astype(F32)
            extra_sum[...] = total

            @pl.when(jnp.logical_not(is_heavy))
            def _():
                extra_copy(heavy_at).start()

    @pl.when(jnp.logical_not(is_heavy))
    def _():
        extra_in[0] = jnp.zeros((rows, LANES), F32)

    tiles_in.wait_recv()
    gradient = chunk_sum[:, mine]
    for d in range(1, n):
        gradient = gradient + tile_in[d]

    @pl.when(is_heavy)
    def _():
        extras_in.wait_recv()
        more = extra_sum[...]
        for d in range(1, n):
            more = more + extra_in[d]
        extra_in[0] = more

    gradient_x = extra_in[0]

    own_state.wait()
    square = gradient * gradient
    square_x = gradient_x * gradient_x

    def new_col(sq, t):
        state = col_state[:, tile(k * per_chunk + t)]
        total = jnp.sum(sq, axis=0, keepdims=True)
        return decay_rate * state + (1.0 - decay_rate) * (total / rows + tiny_term)

    col_new = new_col(square, y)
    col_new_x = new_col(square_x, n)
    half = gradient * lax.rsqrt(col_new)
    half_x = gradient_x * lax.rsqrt(col_new_x)
    both = jnp.concatenate([square + square_x, half * half + half_x * half_x], axis=0)
    sums = lax.dot_general(
        jnp.ones((8, LANES), F32),
        both,
        (((1,), (1,)), ((), ())),
        precision=lax.Precision.HIGHEST,
        preferred_element_type=F32,
    )

    def exchange(stage, members, peer, value):
        stat[stage, 0] = value
        slot = slots.take()
        for d in range(1, members):
            remote(stat.at[stage, 0], stat.at[stage, d], slot, peer(d)).start()
        if members == 1:
            return None
        whole = stat.at[stage, pl.ds(1, members - 1)]
        group = remote(whole, whole, slot, k_peer(1))
        sent.append(group)
        return group

    def collect(stage, members, group, value):
        if group is not None:
            group.wait_recv()
        for d in range(1, members):
            value = value + stat[stage, d]
        return value

    lane = lax.broadcasted_iota(jnp.int32, sums.shape, 1)
    line = lax.broadcasted_iota(jnp.int32, sums.shape, 0)
    state = jnp.where((lane == dp) & (m == 0), jnp.broadcast_to(row_state_ref[...], sums.shape), 0.0)
    sums = jnp.where(line == 1, state, sums)
    stat_group = exchange(0, n, y_peer, sums)

    half_full[:, mine] = half
    half_last = half_full.at[my_rows, last]
    h_slot, hl_slot, hx_slot = slots.take(), slots.take(), slots.take()

    def half_copy(count, slot, d):
        part = half_full.at[pl.ds(0, count), mine]
        return remote(part, part, slot, y_peer(d))

    def half_whole(tiles, count, slot):
        return whole_of(half_full.at[pl.ds(0, count), pl.ds(0, tiles * LANES)], slot)

    @pl.when(is_heavy)
    def _():
        half_full[:, last] = half_x

    for d in (1, n - 1):

        @pl.when(y_of(d) < y_top)
        def _():
            half_copy(top, h_slot, d).start()

        @pl.when(y_of(d) >= y_top)
        def _():
            half_copy(rows, hl_slot, d).start()

    col_chunk[:, mine] = col_new
    ccopy = start_all(
        col_chunk.at[:, seven_tiles],
        lambda slot, d: remote(col_chunk.at[:, mine], col_chunk.at[:, mine], slot, y_peer(d)),
    )
    col_last = col_chunk.at[:, last]
    cx_slot = slots.take()

    @pl.when(is_heavy)
    def _():
        col_chunk[:, last] = col_new_x
        for d in range(1, n):
            remote(col_last, col_last, cx_slot, y_peer(d)).start()

    @pl.when(jnp.logical_not(lower))
    def _():
        master_whole(y_top - 1, body, m_slot).wait_recv()
        master_whole(n - y_top, last, mp_slot).wait_recv()

    @pl.when(lower)
    def _():
        master_whole(y_top, body, m_slot).wait_recv()
        if n - y_top > 1:
            master_whole(n - y_top - 1, last, mp_slot).wait_recv()

    @pl.when(is_heavy)
    def _():
        master_whole(n - 1, last, mx_slot).wait_recv()

    side_tile[0] = half[top:, :]
    side_tile[1] = master_full[top:, mine]
    scopy = start_all(side.at[seven], lambda slot, d: remote(side_tile, side.at[k], slot, k_peer(d)))
    side[k] = side_tile[...]
    sx_slot = slots.take()

    @pl.when(is_heavy)
    def _():
        side_extra[0] = half_x
        side_extra[1] = master_full[:, last]
        for d in range(1, n):
            remote(side_extra, side_extra, sx_slot, k_peer(d)).start()

    sums = collect(0, n, stat_group, sums)
    stat_group = exchange(1, nm, m_peer, sums)
    for d in range(2, n - 1):

        @pl.when(y_of(d) < y_top)
        def _():
            half_copy(top, h_slot, d).start()

        @pl.when(y_of(d) >= y_top)
        def _():
            half_copy(rows, hl_slot, d).start()

    @pl.when(is_heavy)
    def _():
        for d in range(1, n):
            part = half_full.at[pl.ds(pl.multiple_of(y_of(d) * n, n), n), last]
            remote(part, part, hx_slot, y_peer(d)).start()

    ccopy.wait_recv()

    @pl.when(jnp.logical_not(is_heavy))
    def _():
        remote(col_last, col_last, cx_slot, y_peer(1)).wait_recv()

    ocopy = start_all(
        col_out.at[:, seven_chunks],
        lambda slot, d: remote(col_chunk, col_out.at[:, here], slot, k_peer(d)),
    )
    col_out[:, here] = col_chunk[...]
    sums = collect(1, nm, stat_group, sums)
    stat_group = exchange(2, n, k_peer, sums)

    @pl.when(jnp.logical_not(lower))
    def _():
        half_whole(n - 1, top, h_slot).wait_recv()

    @pl.when(lower)
    def _():
        half_whole(n - 1, rows, hl_slot).wait_recv()

    scopy.wait_recv()

    @pl.when(jnp.logical_not(is_heavy))
    def _():
        remote(half_last, half_last, hx_slot, y_peer(1)).wait_recv()
        remote(side_extra, side_extra, sx_slot, k_peer(1)).wait_recv()

    sums = collect(2, n, stat_group, sums)

    row_total = sums[0:1, :rows]
    update_total = sums[0:1, rows:]
    row_state = sums[1:2, :rows]
    row_new = decay_rate * row_state + (1.0 - decay_rate) * (row_total / ff + tiny_term)
    mean_row = jnp.sum(row_new, axis=1, keepdims=True) / rows
    energy = mean_row * jnp.sum(update_total / row_new, axis=1, keepdims=True)
    scale = jnp.maximum(1.0, jnp.sqrt(energy / (rows * ff)) / clip_level)
    factor = lax.rsqrt(row_new) * (step_size * jnp.sqrt(mean_row) / scale)
    eye = lax.broadcasted_iota(jnp.int32, (rows, rows), 0) == lax.broadcasted_iota(jnp.int32, (rows, rows), 1)
    factor = jnp.sum(jnp.where(eye, jnp.broadcast_to(factor, (rows, rows)), 0.0), axis=1, keepdims=True)

    for first, count in bounds:
        where = pl.ds(first * LANES, count * LANES)
        fresh = master_full[:top, where] - factor[:top] * half_full[:top, where]
        weight_out[:top, cols(k * chunk + first * LANES, count * LANES)] = fresh.astype(BF16)
    upper = weight_out.at[pl.ds(0, top), cols(k * chunk, n * LANES)]
    wcopy = start_all(weight_out.at[pl.ds(0, top), pl.ds(0, (n - 1) * n * LANES)], lambda slot, d: remote(upper, upper, slot, k_peer(d)))

    weight_out[:, extra_cols(y)] = (side_extra[1] - factor * side_extra[0]).astype(BF16)
    extra_out = weight_out.at[:, extra_cols(y)]
    xcopy = start_all(weight_out.at[:, seven_tiles], lambda slot, d: remote(extra_out, extra_out, slot, y_peer(d)))

    def side_tile_at(j, yy):
        return tile(j * per_chunk + yy)

    for j in range(n):
        fresh = (side[j, 1] - factor[top:] * side[j, 0]).astype(BF16)
        side_send[:, pl.ds(j * LANES, LANES)] = fresh
        weight_out[top:, side_tile_at(j, y)] = fresh
    ucopy = start_all(side_in.at[others], lambda slot, d: remote(side_send, side_in.at[d], slot, y_peer(d)))

    pick = lax.broadcasted_iota(jnp.int32, (n, rows), 1) - y * n == lax.broadcasted_iota(jnp.int32, (n, rows), 0)
    row_factor = lax.rsqrt(row_new) * (step_size * jnp.sqrt(mean_row) / scale)
    row_factor = jnp.sum(jnp.where(pick, jnp.broadcast_to(row_factor, (n, rows)), 0.0), axis=1, keepdims=True)
    fresh = master_full[my_rows, :] - row_factor * half_full[my_rows, :]
    for r in range(n):
        fresh_rows[r] = fresh[r : r + 1, :]
    fcopy = start_all(master_out.at[:, seven_chunks], lambda slot, d: remote(fresh_rows.at[k_of(d)], master_out.at[:, here], slot, k_peer(d)))
    master_out[:, here] = fresh_rows[k]

    full_lane = lax.broadcasted_iota(jnp.int32, row_new.shape, 1)
    row_out[...] = jnp.sum(jnp.where(full_lane == dp, row_new, 0.0), axis=1, keepdims=True)

    ucopy.wait_recv()
    for d in range(1, n):
        yy = lax.rem(y - d + n, n)
        for j in range(n):
            weight_out[top:, side_tile_at(j, yy)] = side_in[d, :, pl.ds(j * LANES, LANES)]
    ocopy.wait_recv()
    fcopy.wait_recv()
    xcopy.wait_recv()
    wcopy.wait_recv()

    for group in sent:
        group.wait_send()
    tiles_in.wait_send()

    @pl.when(jnp.logical_not(lower))
    def _():
        master_whole(n - 1, body, m_slot).wait_send()
        half_whole(y_top - 1, top, h_slot).wait_send()
        half_whole(n - y_top, rows, hl_slot).wait_send()

    @pl.when(lower)
    def _():
        master_whole(n - 1, last, mp_slot).wait_send()
        half_whole(y_top, top, h_slot).wait_send()
        if n - y_top > 1:
            half_whole(n - y_top - 1, rows, hl_slot).wait_send()

    @pl.when(jnp.logical_not(is_heavy))
    def _():
        master_copy(last, mx_slot, y_peer(1)).wait_send()

    @pl.when(jnp.logical_not(is_heavy))
    def _():
        extra_copy(heavy_at).wait_send()

    @pl.when(is_heavy)
    def _():
        whole_of(half_full.at[pl.ds(0, n), seven_tiles], hx_slot).wait_send()
        remote(col_chunk.at[:, seven_tiles], col_chunk.at[:, seven_tiles], cx_slot, y_peer(1)).wait_send()
        remote(extras_whole, extras_whole, sx_slot, k_peer(1)).wait_send()


def writer(*refs):
    *pairs, sem = refs
    count = len(pairs) // 2
    copies = []
    for a, b in zip(pairs[:count], pairs[count:]):
        step = min(a.shape[0], 16)
        for r in range(0, a.shape[0], step):
            piece = pl.ds(r, step)
            copies.append(pltpu.make_async_copy(a.at[piece], b.at[piece], sem.at[len(copies)]))
    for c in copies:
        c.start()
    for c in copies:
        c.wait()


def build(n, nm, splits):
    def per_device(grad_partials, master, row_state, col_state):
        grad = grad_partials[0]
        rows, width = grad.shape
        chunk = width // n
        quarter = rows // 4
        hbm = pl.BlockSpec(memory_space=pltpu.HBM)
        vmem = pl.BlockSpec(memory_space=pltpu.VMEM)
        dma = pltpu.SemaphoreType.DMA

        def in_hbm(a):
            return pltpu.with_memory_space_constraint(a, pltpu.HBM)

        out = pl.pallas_call(
            functools.partial(kernel, n, nm, splits),
            out_shape=(
                jax.ShapeDtypeStruct((1, width), F32),
                jax.ShapeDtypeStruct((rows, width), BF16),
                jax.ShapeDtypeStruct((1, 1), F32),
                jax.ShapeDtypeStruct((1, width), F32),
            ),
            in_specs=[hbm, hbm, vmem, hbm],
            out_specs=(vmem, vmem, vmem, vmem),
            scratch_shapes=[
                pltpu.VMEM((n, rows, chunk), BF16),
                pltpu.VMEM((rows, chunk), F32),
                pltpu.VMEM((n, rows, LANES), F32),
                pltpu.VMEM((n, rows, LANES), BF16),
                pltpu.VMEM((rows, LANES), F32),
                pltpu.VMEM((2 * n, rows, LANES), F32),
                pltpu.VMEM((n, 1, chunk), F32),
                pltpu.VMEM((rows, chunk), F32),
                pltpu.VMEM((rows, chunk), F32),
                pltpu.VMEM((2, quarter, LANES), F32),
                pltpu.VMEM((2, rows, LANES), F32),
                pltpu.VMEM((n, 2, quarter, LANES), F32),
                pltpu.VMEM((quarter, n * LANES), BF16),
                pltpu.VMEM((n, quarter, n * LANES), BF16),
                pltpu.VMEM((3, max(n, nm), 8, 2 * rows), F32),
                pltpu.VMEM((n, 1, chunk), F32),
                pltpu.VMEM((1, chunk), F32),
                pltpu.VMEM((1, width), F32),
                dma((len(splits) + 3,)),
                dma((27,)),
                dma((27,)),
            ],
            compiler_params=pltpu.CompilerParams(
                collective_id=0, has_side_effects=True, vmem_limit_bytes=32 * 1024 * 1024
            ),
        )(in_hbm(grad), in_hbm(master), row_state.reshape(1, 1), in_hbm(col_state.reshape(1, width)))
        master_new, weight_full, row_new, col_new = pl.pallas_call(
            writer,
            out_shape=tuple(jax.ShapeDtypeStruct(a.shape, a.dtype) for a in out),
            in_specs=[pl.BlockSpec(memory_space=pl.ANY)] * len(out),
            out_specs=tuple([hbm] * len(out)),
            scratch_shapes=[dma((len(out) - 1 + -(-rows // 16),))],
            compiler_params=pltpu.CompilerParams(vmem_limit_bytes=1024 * 1024),
        )(*out)
        return (master_new, weight_full, row_new.reshape(1), col_new.reshape(width))

    return per_device


def solution(mesh):
    in_specs = (P("dp", None, "mp"), P("dp", "mp"), P("dp"), P("mp"))
    out_specs = (P("dp", "mp"), P(None, "mp"), P("dp"), P("mp"))
    return jax.shard_map(
        build(8, 8, (3, 2, 1, 1, 1)), mesh=mesh, in_specs=in_specs, out_specs=out_specs, check_vma=False
    )
```
